256 devices in a mesh: qb: 32 (over y_lo, z, core), kb: 8 (over x, y_hi).
Axes of the slice: x: 4, y: 4 (y_hi: 2, y_lo: 2; y = y_hi * 2 + y_lo), z: 8, core: 2. Of those that a mesh axis runs over, the one named last changes fastest.
Arguments:
- queries: bfloat16 [4, 16384, 128], P(None, 'qb'), may hold values from -100 to 100
- keys: bfloat16 [4, 16384, 128], P(None, ('qb', 'kb')), may hold values from -3.5 to 3.5
- c_proj: bfloat16 [4, 16384, 128], P(None, 'qb'), may hold values from -0.5 to 0.5
- b_proj: bfloat16 [4, 16384, 128], P(None, ('qb', 'kb')), may hold values from -0.5 to 0.5
- decay_rate: float32 [4, 16384], replicated, may hold values from 0 to 1
- doc_ids: int32 [4, 128], replicated, may hold values from 0 to 7, never falling along the last dimension, each value on 1 to 48 neighbouring positions
Outputs:
- grad_c: float32 [4, 16384, 128], P(None, ('qb', 'kb'))
- grad_b: float32 [4, 16384, 128], P(None, ('qb', 'kb'))
- grad_logcum: float32 [4, 16384], P(None, ('qb', 'kb'))
The draws below stay inside these ranges and needn't reach their ends.
Inputs may be any that keep to these rules, and one draw needn't show every extreme that they name: `doc_ids`: within a sequence the numbers never fall; a document covers 1 to 48 blocks.
All inputs are finite; a program needn't handle non-finite values.
Results may differ from the reference program's by a relative error of at most 0.00068.
Values may be sent and summed in bfloat16 or wider, within the bound.
A program may use at most 128 MiB of HBM per device.

```python
import math
import jax
import jax.numpy as jnp
import numpy as np

HD = 128
SEQUENCE_COUNT = 4
TOK_Q = 512
TOKEN_LENGTH = 16384
NBLK = 128
DOCS = 8
DOC_MOST = 48
N_QB = 32


def drawn_keys(key):
    return jnp.clip(jax.random.normal(key, (SEQUENCE_COUNT, TOKEN_LENGTH, HD), jnp.float32), -3.5, 3.5)


def draw_keys(key, part):
    common = drawn_keys(key)
    return common.astype(jnp.bfloat16)


def draw_queries(key, part):
    key = jax.random.fold_in(key, 12)
    single = jnp.clip(jax.random.normal(key, (SEQUENCE_COUNT, TOKEN_LENGTH, HD), jnp.float32), -3.5, 3.5)
    return single.astype(jnp.bfloat16)


def draw_decay_rate(key, part):
    key = jax.random.fold_in(key, 13)
    slow_share = 0.5
    picker = jax.random.uniform(jax.random.fold_in(key, 1), (SEQUENCE_COUNT, 1), jnp.float32) < slow_share
    fast_rate = jnp.exp(jax.random.uniform(jax.random.fold_in(key, 2), (SEQUENCE_COUNT, 1), jnp.float32, math.log(1.0 / 50.0), math.log(1.0 / 30.0)))
    slow_rate = jnp.exp(jax.random.uniform(jax.random.fold_in(key, 3), (SEQUENCE_COUNT, 1), jnp.float32, math.log(0.05 / TOKEN_LENGTH), math.log(0.5 / TOKEN_LENGTH)))
    baseline_rate = jnp.where(picker, slow_rate, fast_rate)
    coarse_grid = jnp.exp(jax.random.uniform(jax.random.fold_in(key, 4), (SEQUENCE_COUNT, TOKEN_LENGTH // 64, 1), jnp.float32, math.log(0.5), math.log(2.0)))
    coarse_grid = jnp.broadcast_to(coarse_grid, (SEQUENCE_COUNT, TOKEN_LENGTH // 64, 64)).reshape(SEQUENCE_COUNT, TOKEN_LENGTH)
    rough_estimate = jax.random.uniform(jax.random.fold_in(key, 5), (SEQUENCE_COUNT, TOKEN_LENGTH), jnp.float32, 0.5, 2.0)
    spike_events = jax.random.bernoulli(jax.random.fold_in(key, 6), 3.0 / TOKEN_LENGTH, (SEQUENCE_COUNT, TOKEN_LENGTH))
    spike_length = jax.random.uniform(jax.random.fold_in(key, 7), (SEQUENCE_COUNT, TOKEN_LENGTH), jnp.float32, 0.22, 0.69)
    return baseline_rate * coarse_grid * rough_estimate + jnp.where(spike_events, spike_length, 0.0)


def steps_of(rng, shape, cuts, least, largest):
    def one(position, shards_of):
        draws = jax.random.uniform(jax.random.fold_in(jax.random.fold_in(rng, 6), position), (shards_of,), jnp.float32, least / len(cuts), largest / len(cuts))
        return jnp.repeat(jnp.exp(draws), shape[position] // shards_of).reshape((-1,) + (1,) * (len(shape) - position - 1))

    factor_of = one(*cuts[0])
    for cut in cuts[1:]:
        factor_of = factor_of * one(*cut)
    return factor_of


def profile(count, total, bound, skew):
    loads = [(1 << 20) // math.isqrt(rank ** skew) + 1 for rank in range(2, count + 1)]
    spare, holding = total - bound - (count - 1), [1] * (count - 1)
    while spare > 0:
        free = [i for i in range(count - 1) if holding[i] < bound]
        mass, remaining = sum([loads[i] for i in free]), spare
        for i in free:
            extra = min(bound - holding[i], max(1, remaining * loads[i] // mass), spare)
            holding[i] = holding[i] + extra
            spare = spare - extra
    return np.array([bound] + holding)


def uneven_parts(rng, amount, total, most, slope):
    if amount == 2:
        one = jax.random.randint(rng, (), max(1, total - most), min(most, total - 1) + 1)
        return jnp.stack([one, total - one])
    sizes = jnp.asarray(profile(amount, total, most, slope), jnp.int32)
    couples = (amount - 1) // 2
    source_of, sink = sizes[1:1 + 2 * couples:2], sizes[2:2 + 2 * couples:2]
    margin = jnp.minimum(source_of - 1, most - sink)
    moved = jax.random.randint(jax.random.fold_in(rng, 1), (couples,), 0, 1 << 20) % (margin + 1)
    sizes = sizes.at[1:1 + 2 * couples:2].set(source_of - moved).at[2:2 + 2 * couples:2].set(sink + moved)
    return sizes[jax.random.permutation(jax.random.fold_in(rng, 2), amount)]


def normal_values(key, extent, deviation, most, shards=(), kind=jnp.bfloat16):
    level = steps_of(key, extent, shards, -0.22, 0.18) if shards else 1.0
    result = jax.random.normal(key, extent, jnp.float32) * deviation * level
    return jnp.minimum(jnp.maximum(result, -most), most).astype(kind)


def setup_inputs(seed: int = 0) -> dict:
    arg_keys = jax.random.split(jax.random.key(seed), 7)
    return {
        "queries": draw_queries(jax.random.fold_in(arg_keys[6], 71), 0),
        "keys": draw_keys(jax.random.fold_in(arg_keys[6], 71), 0),
        "c_proj": normal_values(arg_keys[2], (SEQUENCE_COUNT, TOKEN_LENGTH, HD), HD ** -0.5, 0.5, ((1, 32),)),
        "b_proj": normal_values(arg_keys[3], (SEQUENCE_COUNT, TOKEN_LENGTH, HD), HD ** -0.5, 0.5, ((1, 256),)),
        "decay_rate": draw_decay_rate(jax.random.fold_in(arg_keys[6], 71), 0),
        "doc_ids": jax.vmap(lambda own: jnp.searchsorted(jnp.cumsum(uneven_parts(own, DOCS, NBLK, DOC_MOST, 0)), jnp.arange(NBLK), side="right"))(jax.random.split(arg_keys[5], SEQUENCE_COUNT)).reshape((SEQUENCE_COUNT, NBLK)).astype(jnp.int32),
    }


NEGATIVE = -1.0e30


def reference(queries, keys, c_proj, b_proj, decay_rate, doc_ids):
    score_scale = HD ** -0.5
    logcum = jnp.cumsum(-decay_rate, axis=1)
    documents = jnp.repeat(doc_ids, 128, axis=1)
    positions = jnp.arange(TOKEN_LENGTH, dtype=jnp.int32)
    keys_wide = keys.astype(jnp.float32)
    bproj_wide = b_proj.astype(jnp.float32)
    grad_b = jnp.zeros((SEQUENCE_COUNT, TOKEN_LENGTH, HD), jnp.float32)
    col_flow = jnp.zeros((SEQUENCE_COUNT, TOKEN_LENGTH), jnp.float32)
    grad_c_parts = []
    row_flow_parts = []
    for row_block in range(N_QB):
        start_row = row_block * TOK_Q
        end_row = start_row + TOK_Q
        query_rows = queries[:, start_row:end_row].astype(jnp.float32)
        cproj_rows = c_proj[:, start_row:end_row].astype(jnp.float32)
        scores = jnp.einsum("srd,skd->srk", query_rows, keys_wide[:, :end_row]) * score_scale
        allowed = (positions[None, None, :end_row] <= positions[None, start_row:end_row, None]) & (
            documents[:, None, :end_row] == documents[:, start_row:end_row, None])
        masked = jnp.where(allowed, scores, NEGATIVE)
        row_top = jnp.max(masked, axis=2, keepdims=True)
        exponent = jnp.where(allowed, jnp.exp(masked - row_top), 0.0)
        attention = exponent / jnp.sum(exponent, axis=2, keepdims=True)
        products = jnp.einsum("srd,skd->srk", cproj_rows, bproj_wide[:, :end_row])
        spread = jnp.where(allowed, logcum[:, start_row:end_row, None] - logcum[:, None, :end_row], 0.0)
        decay_tile = jnp.where(allowed, jnp.exp(spread), 0.0)
        mixing = products * decay_tile
        twice_gap = jnp.where(allowed, 2.0 * (mixing - attention), 0.0)
        weighted = (twice_gap * decay_tile).astype(jnp.bfloat16).astype(jnp.float32)
        grad_c_parts.append(jnp.einsum("srk,skd->srd", weighted, bproj_wide[:, :end_row]))
        grad_b = grad_b.at[:, :end_row].add(jnp.einsum("srk,srd->skd", weighted, cproj_rows))
        flow_tile = twice_gap * mixing
        row_flow_parts.append(jnp.sum(flow_tile, axis=2))
        col_flow = col_flow.at[:, :end_row].add(jnp.sum(flow_tile, axis=1))
    grad_c = jnp.concatenate(grad_c_parts, axis=1)
    row_flow = jnp.concatenate(row_flow_parts, axis=1)
    return grad_c, grad_b, row_flow - col_flow
```

```python
import functools
import math

import jax
import jax.numpy as jnp
from jax import lax
from jax.experimental import pallas as pl
from jax.experimental.pallas import tpu as pltpu
from jax.sharding import PartitionSpec as P

MESH = pl.DeviceIdType.MESH
NEG = -1e30
SK = 64
BLK = 128
SLOTS = 7


def nt(a, b, precision=None):
    return lax.dot_general(
        a, b, (((1,), (1,)), ((), ())), preferred_element_type=jnp.float32, precision=precision
    )


def kernel(
    nq, nk,
    q_ref, c_ref, k_ref, b_ref, lc_ref, doc_ref,
    gc_ref, gb_ref, gl_ref,
    kbuf, bbuf, ebuf, mbuf, lbuf, fbuf, lckb, gct, rf, gp, sib, up, dn, gcp, gcr, st, str_, cf,
    ks, kr, bs, br, kss, ksr, bss, bsr, sts, strs, gss, gsr, us, ur, ds, dr, gcs, gcrs,
):
    S, R, D = q_ref.shape
    RB = R // BLK
    NROW = S * SK
    npair = nq // 2
    qb = lax.axis_index("qb")
    kb = lax.axis_index("kb")
    pr = qb // 2
    core = qb % 2
    other = 1 - core
    kblk = (kb * SK) // BLK
    khalf = kb % 2

    def dev(step):
        return (((pr + step + npair) % npair) * 2 + core, kb)

    nxt, prv, far, back = dev(1), dev(-1), dev(6), dev(-6)
    sibling = (pr * 2 + other, kb)
    peers = [(qb, (kb + o) % nk) for o in range(1, nk)]

    def rc(src, dst, ssem, rsem, to):
        return pltpu.make_async_remote_copy(
            src_ref=src, dst_ref=dst, send_sem=ssem, recv_sem=rsem, device_id=to, device_id_type=MESH
        )

    def ring(own, buf, ssem, rsem):
        def src(e):
            return own if e == 0 else buf.at[e, :, core]

        plan = {1: (0, nxt), 2: (1, nxt), 3: (2, nxt), 6: (0, far), 5: (6, prv), 4: (5, prv)}
        return {e: rc(src(f), buf.at[e, :, core], ssem.at[e], rsem.at[e], to) for e, (f, to) in plan.items()}

    def pair_up(own, buf, ssem, rsem):
        out = []
        for e in range(SLOTS):
            src = own if e == 0 else buf.at[e, :, core]
            out.append((
                rc(src, buf.at[e, :, core], ssem.at[e], rsem.at[e], sibling),
                rc(buf.at[e, :, other], buf.at[e, :, other], ssem.at[e], rsem.at[e], sibling),
            ))
        return out

    kc = ring(k_ref, kbuf, ks, kr)
    bc = ring(b_ref, bbuf, bs, br)
    kx = pair_up(k_ref, kbuf, kss, ksr)
    bx = pair_up(b_ref, bbuf, bss, bsr)

    barrier = pltpu.get_barrier_semaphore()
    partners = [nxt, prv, far, back, sibling] + peers
    for to in partners:
        pl.semaphore_signal(barrier, inc=1, device_id=to, device_id_type=MESH)
    pl.semaphore_wait(barrier, len(partners))

    kc[1].start()
    kc[6].start()
    kx[0][0].start()

    lane = lax.broadcasted_iota(jnp.int32, (1, BLK), 1)
    sub = lax.broadcasted_iota(jnp.int32, (BLK, BLK), 0)

    def key_block(e, u):
        j = (pr - e + npair) % npair
        return (2 * j + u) * RB + kblk

    def biases(e, s, r):
        rd = doc_ref[s, qb * RB + r]
        out = []
        for u in range(2):
            kd = doc_ref[s, key_block(e, u)]
            same = kd == rd
            if e:
                same = same & (pr >= e)
            out.append(jnp.where(same, 0.0, NEG).astype(jnp.float32))
        return out

    def causal(r):
        kpos = (2 * pr) * R + kb * SK + jnp.where(sub >= SK, sub - SK + R, sub)
        rpos = qb * R + r * BLK + lane
        return kpos <= rpos

    kbuf[0, :, core] = k_ref[...]
    bbuf[0, :, core] = b_ref[...]
    gct[...] = jnp.zeros_like(gct)
    rf[...] = jnp.zeros_like(rf)
    gp[:, :, NROW:, :] = jnp.zeros((SLOTS, 2, 8, D), jnp.float32)
    gcp[:, NROW:, :] = jnp.zeros((nk, 8, D), jnp.float32)

    def key_columns(e):
        def body(s, _):
            first = lc_ref[s, pl.ds(key_block(e, 0), 1), :]
            second = lc_ref[s, pl.ds(key_block(e, 1), 1), :]
            low = jnp.concatenate([first[:, :SK], second[:, :SK]], axis=1)
            high = jnp.concatenate([first[:, SK:], second[:, SK:]], axis=1)
            row = jnp.where(jnp.full((1, BLK), khalf) == 0, low, high)
            lckb[e, s] = jnp.broadcast_to(row, (BLK, BLK)).T
            return 0

        lax.fori_loop(0, S, body, 0)

    scale = (D ** -0.5) * math.log2(math.e)

    def first_pass(e):
        def body(s, _):
            keys = kbuf[e, s].reshape(BLK, D)
            for r in range(RB):
                cols = slice(r * BLK, (r + 1) * BLK)
                sc = nt(keys, q_ref[s, cols, :]) * scale
                if e == 0:
                    sc = jnp.where(causal(r), sc, NEG)
                bias = biases(e, s, r)
                halves = [sc[:SK], sc[SK:]]
                top = jnp.maximum(
                    jnp.max(halves[0], axis=0, keepdims=True) + bias[0],
                    jnp.max(halves[1], axis=0, keepdims=True) + bias[1],
                )
                total = jnp.zeros((1, BLK), jnp.float32)
                for u in range(2):
                    ex = jnp.exp2(halves[u] - jnp.maximum(top, NEG - 2.0 * bias[u]))
                    ebuf[e, s, u * SK:(u + 1) * SK, cols] = ex
                    total += jnp.sum(ex, axis=0, keepdims=True)
                mbuf[e, s, :, cols] = top
                lbuf[e, s, :, cols] = total
            return 0

        lax.fori_loop(0, S, body, 0)

    key_columns(0)
    key_columns(1)
    kc[1].wait_recv()
    kc[2].start()
    kx[1][0].start()
    kc[6].wait_recv()
    kc[5].start()
    kx[6][0].start()
    bc[1].start()
    bc[6].start()
    bx[0][0].start()
    kx[0][1].wait_recv()
    first_pass(0)
    kx[1][1].wait_recv()
    first_pass(1)
    kc[2].wait_recv()
    kc[3].start()
    kx[2][0].start()
    kc[5].wait_recv()
    kc[4].start()
    kx[5][0].start()
    kx[6][1].wait_recv()
    first_pass(6)
    kx[2][1].wait_recv()
    first_pass(2)
    kx[5][1].wait_recv()
    first_pass(5)
    bc[1].wait_recv()
    bc[2].start()
    bx[1][0].start()
    bc[6].wait_recv()
    bc[5].start()
    bx[6][0].start()
    kc[3].wait_recv()
    kx[3][0].start()
    kc[4].wait_recv()
    kx[4][0].start()
    for e in range(2, SLOTS):
        key_columns(e)
    kx[3][1].wait_recv()
    first_pass(3)
    kx[4][1].wait_recv()
    first_pass(4)

    top = mbuf[0]
    for e in range(1, SLOTS):
        top = jnp.maximum(top, mbuf[e])
    total = jnp.zeros_like(top)
    for e in range(SLOTS):
        total += lbuf[e] * jnp.exp2(mbuf[e] - top)
    st[0] = top
    st[1] = total
    stats = [rc(st, str_.at[o], sts.at[o], strs.at[o], peers[o - 1]) for o in range(1, nk)]
    for copy in stats:
        copy.start()
    bc[2].wait_recv()
    bc[3].start()
    bx[2][0].start()
    bc[5].wait_recv()
    bc[4].start()
    bx[5][0].start()
    for copy in stats:
        copy.wait_recv()
    best = top
    for o in range(1, nk):
        best = jnp.maximum(best, str_[o, 0])
    whole = total * jnp.exp2(top - best)
    for o in range(1, nk):
        whole += str_[o, 1] * jnp.exp2(str_[o, 0] - best)
    for e in range(SLOTS):
        fbuf[e] = jnp.exp2(mbuf[e] - best) / whole

    ones = jnp.ones((8, BLK), jnp.float32)

    def second_pass(e):
        def body(s, _):
            bb = bbuf[e, s].reshape(BLK, D)
            bt = bb.T
            kcol = lckb[e, s]
            weights = []
            gathered = jnp.zeros((BLK, BLK), jnp.float32)
            for r in range(RB):
                cols = slice(r * BLK, (r + 1) * BLK)
                prod = nt(bb, c_ref[s, cols, :])
                bias = biases(e, s, r)
                rows = lc_ref[s, pl.ds(qb * RB + r, 1), :]
                spread = jnp.concatenate(
                    [(rows + bias[0]) - kcol[:SK], (rows + bias[1]) - kcol[SK:]], axis=0
                )
                if e == 0:
                    spread = jnp.where(causal(r), spread, NEG)
                decay = jnp.exp(spread)
                mixing = prod * decay
                gap = mixing - ebuf[e, s, :, cols] * fbuf[e, s, :, cols]
                flow = gap * mixing
                w = (gap * decay).astype(jnp.bfloat16)
                weights.append(w)
                gathered += flow
                rf[s, :, cols] += jnp.sum(flow.reshape(BLK // 8, 8, BLK), axis=0)
                gct[s, :, cols] += jnp.dot(bt, w, preferred_element_type=jnp.float32)
            w = jnp.concatenate(weights, axis=1)
            part = jnp.dot(w, c_ref[s], preferred_element_type=jnp.float32)
            colf = nt(ones, gathered, lax.Precision.HIGHEST)[0:1]
            rows = pl.ds(pl.multiple_of(s * SK, SK), SK)
            for u in range(2):
                gp[e, u, rows, :] = part[u * SK:(u + 1) * SK]
            cf[s] = colf
            return 0

        lax.fori_loop(0, S, body, 0)
        for s in range(S):
            for u in range(2):
                gp[e, u, NROW + s:NROW + s + 1, :] = cf[s]

    gx = [rc(gp.at[e, other], sib.at[e], gss.at[e], gsr.at[e], sibling) for e in range(SLOTS)]
    uc = [rc(gp.at[e, core], up.at[i], us.at[i], ur.at[i], prv) for i, e in enumerate((3, 2, 1))]
    dc = [
        rc(gp.at[e, core], dn.at[i], ds.at[i], dr.at[i], to)
        for i, (e, to) in enumerate(((4, nxt), (5, nxt), (6, back)))
    ]

    def grads(e):
        bx[e][1].wait_recv()
        second_pass(e)
        gx[e].start()

    def send_up(i):
        e = 3 - i
        gx[e].wait_recv()
        if i:
            uc[i - 1].wait_recv()
            gp[e, core] = gp[e, core] + sib[e] + up[i - 1]
        else:
            gp[e, core] = gp[e, core] + sib[e]
        uc[i].start()

    def send_dn(i):
        e = 4 + i
        gx[e].wait_recv()
        if i:
            dc[i - 1].wait_recv()
            gp[e, core] = gp[e, core] + sib[e] + dn[i - 1]
        else:
            gp[e, core] = gp[e, core] + sib[e]
        dc[i].start()

    bc[3].wait_recv()
    bx[3][0].start()
    bc[4].wait_recv()
    bx[4][0].start()
    grads(3)
    grads(4)
    send_up(0)
    send_dn(0)
    grads(5)
    grads(2)
    send_dn(1)
    send_up(1)
    grads(6)
    grads(1)
    send_dn(2)
    send_up(2)
    grads(0)

    def spread_c(s, _):
        turned = gct[s].T
        rows = pl.ds(pl.multiple_of(s * SK, SK), SK)
        for o in range(nk):
            gcp[o, rows, :] = turned[o * SK:(o + 1) * SK]
        return 0

    lax.fori_loop(0, S, spread_c, 0)
    for s in range(S):
        flows = jnp.sum(rf[s], axis=0, keepdims=True)
        for o in range(nk):
            g = (o * SK) // BLK
            gcp[o, NROW + s:NROW + s + 1, :] = flows[:, g * BLK:(g + 1) * BLK]
    cc = [
        rc(gcp.at[(kb + o) % nk], gcr.at[o], gcs.at[o], gcrs.at[o], peers[o - 1])
        for o in range(1, nk)
    ]
    for copy in cc:
        copy.start()

    gx[0].wait_recv()
    uc[2].wait_recv()
    dc[2].wait_recv()
    bsum = (gp[0, core] + sib[0]) + (up[2] + dn[2])
    for copy in cc:
        copy.wait_recv()
    csum = gcp[kb]
    for o in range(1, nk):
        csum += gcr[o]
    bsum = bsum * 2.0
    csum = csum * 2.0
    for s in range(S):
        gb_ref[s] = bsum[s * SK:(s + 1) * SK]
        gc_ref[s] = csum[s * SK:(s + 1) * SK]
    rowf = csum[NROW:NROW + S]
    colf = bsum[NROW:NROW + S]
    rowf = jnp.where(jnp.full((S, SK), khalf) == 0, rowf[:, :SK], rowf[:, SK:])
    colf = jnp.where(jnp.full((S, SK), core) == 0, colf[:, :SK], colf[:, SK:])
    gl_ref[...] = rowf - colf

    for e in range(SLOTS):
        kx[e][0].wait_send()
        bx[e][0].wait_send()
        gx[e].wait_send()
        if e:
            kc[e].wait_send()
            bc[e].wait_send()
    for copy in stats + uc + dc + cc:
        copy.wait_send()


def shards(nq, nk, queries, keys, c_proj, b_proj, decay_rate, doc_ids):
    S, R, D = queries.shape
    logcum = jnp.cumsum(-decay_rate, axis=1).reshape(S, -1, BLK)
    pay = S * SK + 8
    vmem = pl.BlockSpec(memory_space=pltpu.VMEM)
    dma = pltpu.SemaphoreType.DMA
    f32, bf16 = jnp.float32, jnp.bfloat16
    return pl.pallas_call(
        functools.partial(kernel, nq, nk),
        out_shape=(
            jax.ShapeDtypeStruct((S, SK, D), f32),
            jax.ShapeDtypeStruct((S, SK, D), f32),
            jax.ShapeDtypeStruct((S, SK), f32),
        ),
        in_specs=[vmem] * 5 + [pl.BlockSpec(memory_space=pltpu.SMEM)],
        out_specs=(vmem, vmem, vmem),
        scratch_shapes=[
            pltpu.VMEM((SLOTS, S, 2, SK, D), bf16),
            pltpu.VMEM((SLOTS, S, 2, SK, D), bf16),
            pltpu.VMEM((SLOTS, S, BLK, R), f32),
            pltpu.VMEM((SLOTS, S, 1, R), f32),
            pltpu.VMEM((SLOTS, S, 1, R), f32),
            pltpu.VMEM((SLOTS, S, 1, R), f32),
            pltpu.VMEM((SLOTS, S, BLK, BLK), f32),
            pltpu.VMEM((S, D, R), f32),
            pltpu.VMEM((S, 8, R), f32),
            pltpu.VMEM((SLOTS, 2, pay, D), f32),
            pltpu.VMEM((SLOTS, pay, D), f32),
            pltpu.VMEM((3, pay, D), f32),
            pltpu.VMEM((3, pay, D), f32),
            pltpu.VMEM((nk, pay, D), f32),
            pltpu.VMEM((nk, pay, D), f32),
            pltpu.VMEM((2, S, 1, R), f32),
            pltpu.VMEM((nk, 2, S, 1, R), f32),
            pltpu.VMEM((S, 1, BLK), f32),
        ]
        + [dma((SLOTS,))] * 8
        + [dma((nk,))] * 2
        + [dma((SLOTS,))] * 2
        + [dma((3,))] * 4
        + [dma((nk,))] * 2,
        compiler_params=pltpu.CompilerParams(
            collective_id=0, has_side_effects=True, vmem_limit_bytes=48 * 1024 * 1024
        ),
    )(queries, c_proj, keys, b_proj, logcum, doc_ids)


def solution(mesh):
    placed = (
        P(None, "qb", None),
        P(None, ("qb", "kb"), None),
        P(None, "qb", None),
        P(None, ("qb", "kb"), None),
        P(),
        P(),
    )
    return jax.shard_map(
        functools.partial(shards, mesh.shape["qb"], mesh.shape["kb"]),
        mesh=mesh,
        in_specs=placed,
        out_specs=(P(None, ("qb", "kb"), None), P(None, ("qb", "kb"), None), P(None, ("qb", "kb"))),
        check_vma=False,
    )
```

```python
import functools
import math

import jax
import jax.numpy as jnp
from jax import lax
from jax.experimental import pallas as pl
from jax.experimental.pallas import tpu as pltpu
from jax.sharding import PartitionSpec as P

MESH = pl.DeviceIdType.MESH
NEG = -1e30
SK = 64
BLK = 128
SLOTS = 7


def nt(a, b, precision=None):
    return lax.dot_general(
        a, b, (((1,), (1,)), ((), ())), preferred_element_type=jnp.float32, precision=precision
    )


def kernel(
    nq, nk,
    q_ref, c_ref, k_ref, b_ref, lc_ref, doc_ref,
    gc_ref, gb_ref, gl_ref,
    kbuf, bbuf, ebuf, mbuf, lbuf, fbuf, lckb, gct, rf, gp, sib, up, dn, gcp, gcr, st, str_,
    ks, kr, bs, br, kss, ksr, bss, bsr, sts, strs, gss, gsr, us, ur, ds, dr, gcs, gcrs,
):
    S, R, D = q_ref.shape
    RB = R // BLK
    HS = S // 2
    NROW = HS * SK
    npair = nq // 2
    qb = lax.axis_index("qb")
    kb = lax.axis_index("kb")
    pr = qb // 2
    core = qb % 2
    other = 1 - core
    kblk = (kb * SK) // BLK
    khalf = kb % 2

    def dev(step):
        return (((pr + step + npair) % npair) * 2 + core, kb)

    nxt, prv, far, back = dev(1), dev(-1), dev(6), dev(-6)
    sibling = (pr * 2 + other, kb)
    peers = [(qb, (kb + o) % nk) for o in range(1, nk)]

    def rc(src, dst, ssem, rsem, to):
        return pltpu.make_async_remote_copy(
            src_ref=src, dst_ref=dst, send_sem=ssem, recv_sem=rsem, device_id=to, device_id_type=MESH
        )

    def ring(own, buf, ssem, rsem):
        def src(e):
            return own if e == 0 else buf.at[e, :, core]

        plan = {1: (0, nxt), 2: (1, nxt), 3: (2, nxt), 6: (0, far), 5: (6, prv), 4: (5, prv)}
        return {e: rc(src(f), buf.at[e, :, core], ssem.at[e], rsem.at[e], to) for e, (f, to) in plan.items()}

    def pair_up(own, buf, ssem, rsem):
        out = []
        for e in range(SLOTS):
            src = own if e == 0 else buf.at[e, :, core]
            out.append((
                rc(src, buf.at[e, :, core], ssem.at[e], rsem.at[e], sibling),
                rc(buf.at[e, :, other], buf.at[e, :, other], ssem.at[e], rsem.at[e], sibling),
            ))
        return out

    kc = ring(k_ref, kbuf, ks, kr)
    bc = ring(b_ref, bbuf, bs, br)
    kx = pair_up(k_ref, kbuf, kss, ksr)
    bx = pair_up(b_ref, bbuf, bss, bsr)

    barrier = pltpu.get_barrier_semaphore()
    partners = [nxt, prv, far, back, sibling] + peers
    for to in partners:
        pl.semaphore_signal(barrier, inc=1, device_id=to, device_id_type=MESH)
    pl.semaphore_wait(barrier, len(partners))

    kc[1].start()
    kc[6].start()
    kx[0][0].start()
    bc[1].start()
    bc[6].start()
    bx[0][0].start()

    lane = lax.broadcasted_iota(jnp.int32, (1, BLK), 1)
    sub = lax.broadcasted_iota(jnp.int32, (BLK, BLK), 0)

    def key_block(e, u):
        j = (pr - e + npair) % npair
        return (2 * j + u) * RB + kblk

    def biases(e, s, r):
        rd = doc_ref[s, qb * RB + r]
        out = []
        for u in range(2):
            kd = doc_ref[s, key_block(e, u)]
            same = kd == rd
            if e:
                same = same & (pr >= e)
            out.append(jnp.where(same, 0.0, NEG).astype(jnp.float32))
        return out

    def causal(r):
        kpos = (2 * pr) * R + kb * SK + jnp.where(sub >= SK, sub - SK + R, sub)
        rpos = qb * R + r * BLK + lane
        return kpos <= rpos

    kbuf[0, :, core] = k_ref[...]
    bbuf[0, :, core] = b_ref[...]
    gct[...] = jnp.zeros_like(gct)
    rf[...] = jnp.zeros_like(rf)
    gp[:, :, :, NROW:, :] = jnp.zeros((SLOTS, 2, 2, 8, D), jnp.float32)
    gcp[:, :, NROW:, :] = jnp.zeros((nk, 2, 8, D), jnp.float32)

    def key_columns(e):
        def body(s, _):
            first = lc_ref[s, pl.ds(key_block(e, 0), 1), :]
            second = lc_ref[s, pl.ds(key_block(e, 1), 1), :]
            low = jnp.concatenate([first[:, :SK], second[:, :SK]], axis=1)
            high = jnp.concatenate([first[:, SK:], second[:, SK:]], axis=1)
            row = jnp.where(jnp.full((1, BLK), khalf) == 0, low, high)
            lckb[e, s] = jnp.broadcast_to(row, (BLK, BLK)).T
            return 0

        lax.fori_loop(0, S, body, 0, unroll=True)

    scale = (D ** -0.5) * math.log2(math.e)

    def first_pass(e):
        def body(s, _):
            every = nt(kbuf[e, s].reshape(BLK, D), q_ref[s]) * scale
            for r in range(RB):
                cols = slice(r * BLK, (r + 1) * BLK)
                sc = every[:, cols]
                if e == 0:
                    sc = jnp.where(causal(r), sc, NEG)
                bias = biases(e, s, r)
                halves = [sc[:SK], sc[SK:]]
                top = jnp.maximum(
                    jnp.max(halves[0], axis=0, keepdims=True) + bias[0],
                    jnp.max(halves[1], axis=0, keepdims=True) + bias[1],
                )
                total = jnp.zeros((1, BLK), jnp.float32)
                for u in range(2):
                    ex = jnp.exp2(halves[u] - jnp.maximum(top, NEG - 2.0 * bias[u]))
                    ebuf[e, s, u * SK:(u + 1) * SK, cols] = ex
                    total += jnp.sum(ex, axis=0, keepdims=True)
                mbuf[e, s, :, cols] = top
                lbuf[e, s, :, cols] = total
            return 0

        lax.fori_loop(0, S, body, 0, unroll=True)

    def passed(copies, siblings, e, follow=None):
        copies[e].wait_recv()
        if follow is not None:
            copies[follow].start()
        siblings[e][0].start()

    def scored(e):
        kx[e][1].wait_recv()
        first_pass(e)

    for e in range(SLOTS):
        key_columns(e)
    scored(0)
    passed(kc, kx, 1, 2)
    passed(bc, bx, 1, 2)
    scored(1)
    passed(kc, kx, 6, 5)
    passed(kc, kx, 2, 3)
    passed(bc, bx, 6, 5)
    passed(bc, bx, 2, 3)
    scored(6)
    scored(2)
    passed(kc, kx, 5, 4)
    passed(kc, kx, 3)
    scored(5)
    scored(3)
    passed(bc, bx, 5, 4)
    passed(bc, bx, 3)
    passed(kc, kx, 4)
    scored(4)

    top = mbuf[0]
    for e in range(1, SLOTS):
        top = jnp.maximum(top, mbuf[e])
    total = jnp.zeros_like(top)
    for e in range(SLOTS):
        total += lbuf[e] * jnp.exp2(mbuf[e] - top)
    st[0] = top
    st[1] = total
    stats = [rc(st, str_.at[o], sts.at[o], strs.at[o], peers[o - 1]) for o in range(1, nk)]
    for copy in stats:
        copy.start()
    passed(bc, bx, 4)
    for copy in stats:
        copy.wait_recv()
    best = top
    for o in range(1, nk):
        best = jnp.maximum(best, str_[o, 0])
    whole = total * jnp.exp2(top - best)
    for o in range(1, nk):
        whole += str_[o, 1] * jnp.exp2(str_[o, 0] - best)
    for e in range(SLOTS):
        fbuf[e] = jnp.exp2(mbuf[e] - best) / whole

    ones = jnp.ones((8, BLK), jnp.float32)

    def second_pass(h, e, i):
        s = h * HS + i
        bb = bbuf[e, s].reshape(BLK, D)
        bt = bb.T
        kcol = lckb[e, s]
        products = nt(bb, c_ref[s])
        weights = []
        gathered = jnp.zeros((BLK, BLK), jnp.float32)
        for r in range(RB):
            cols = slice(r * BLK, (r + 1) * BLK)
            bias = biases(e, s, r)
            rows = lc_ref[s, pl.ds(qb * RB + r, 1), :]
            spread = jnp.concatenate(
                [(rows + bias[0]) - kcol[:SK], (rows + bias[1]) - kcol[SK:]], axis=0
            )
            if e == 0:
                spread = jnp.where(causal(r), spread, NEG)
            decay = jnp.exp(spread)
            mixing = products[:, cols] * decay
            gap = mixing - ebuf[e, s, :, cols] * fbuf[e, s, :, cols]
            flow = gap * mixing
            weights.append((gap * decay).astype(jnp.bfloat16))
            gathered += flow
            rf[s, :, cols] += jnp.sum(flow.reshape(BLK // 8, 8, BLK), axis=0)
        w = jnp.concatenate(weights, axis=1)
        gct[s] += jnp.dot(bt, w, preferred_element_type=jnp.float32)
        part = jnp.dot(w, c_ref[s], preferred_element_type=jnp.float32)
        colf = nt(ones, gathered, lax.Precision.HIGHEST)[0:1]
        for u in range(2):
            gp[e, u, h, i * SK:(i + 1) * SK, :] = part[u * SK:(u + 1) * SK]
            gp[e, u, h, NROW + i:NROW + i + 1, :] = colf

    both = range(2)
    gx = [
        [rc(gp.at[e, other, h], sib.at[e, h], gss.at[e, h], gsr.at[e, h], sibling) for h in both]
        for e in range(SLOTS)
    ]
    uc = [
        [rc(gp.at[e, core, h], up.at[i, h], us.at[i, h], ur.at[i, h], prv) for h in both]
        for i, e in enumerate((3, 2, 1))
    ]
    dc = [
        [rc(gp.at[e, core, h], dn.at[i, h], ds.at[i, h], dr.at[i, h], to) for h in both]
        for i, (e, to) in enumerate(((4, nxt), (5, nxt), (6, back)))
    ]
    cc = [
        [rc(gcp.at[(kb + o) % nk, h], gcr.at[o, h], gcs.at[o, h], gcrs.at[o, h], peers[o - 1]) for h in both]
        for o in range(1, nk)
    ]

    def grads(h, *slots):
        for e in slots:
            if h == 0:
                bx[e][1].wait_recv()
        for e in slots:
            for i in range(HS):
                second_pass(h, e, i)
        for e in slots:
            gx[e][h].start()

    def chain(h, step):
        for e, copies, landed in ((4 + step, dc, dn), (3 - step, uc, up)):
            gx[e][h].wait_recv()
            if step:
                copies[step - 1][h].wait_recv()
                gp[e, core, h] = gp[e, core, h] + sib[e, h] + landed[step - 1, h]
            else:
                gp[e, core, h] = gp[e, core, h] + sib[e, h]
            copies[step][h].start()

    def spread_c(h):
        for i in range(HS):
            s = h * HS + i
            turned = gct[s].T
            flows = jnp.sum(rf[s], axis=0, keepdims=True)
            for o in range(nk):
                g = (o * SK) // BLK
                gcp[o, h, i * SK:(i + 1) * SK, :] = turned[o * SK:(o + 1) * SK]
                gcp[o, h, NROW + i:NROW + i + 1, :] = flows[:, g * BLK:(g + 1) * BLK]
        for copies in cc:
            copies[h].start()

    def finish(h):
        gx[0][h].wait_recv()
        uc[2][h].wait_recv()
        dc[2][h].wait_recv()
        bsum = ((gp[0, core, h] + sib[0, h]) + (up[2, h] + dn[2, h])) * 2.0
        for copies in cc:
            copies[h].wait_recv()
        csum = gcp[kb, h]
        for o in range(1, nk):
            csum += gcr[o, h]
        csum = csum * 2.0
        for i in range(HS):
            s = h * HS + i
            gb_ref[s] = bsum[i * SK:(i + 1) * SK]
            gc_ref[s] = csum[i * SK:(i + 1) * SK]
        rowf = csum[NROW:NROW + HS]
        colf = bsum[NROW:NROW + HS]
        rowf = jnp.where(jnp.full((HS, SK), khalf) == 0, rowf[:, :SK], rowf[:, SK:])
        colf = jnp.where(jnp.full((HS, SK), core) == 0, colf[:, :SK], colf[:, SK:])
        gl_ref[h * HS:(h + 1) * HS] = rowf - colf

    grads(0, 3, 4)
    grads(0, 2, 5)
    chain(0, 0)
    grads(0, 1, 6)
    grads(0, 0)
    spread_c(0)
    grads(1, 3, 4)
    grads(1, 2, 5)
    chain(1, 0)
    chain(0, 1)
    grads(1, 1, 6)
    grads(1, 0)
    spread_c(1)
    chain(1, 1)
    chain(0, 2)
    chain(1, 2)
    finish(0)
    finish(1)

    for e in range(SLOTS):
        kx[e][0].wait_send()
        bx[e][0].wait_send()
        if e:
            kc[e].wait_send()
            bc[e].wait_send()
    for copy in stats:
        copy.wait_send()
    for copies in gx + uc + dc + cc:
        for copy in copies:
            copy.wait_send()


def shards(nq, nk, queries, keys, c_proj, b_proj, decay_rate, doc_ids):
    S, R, D = queries.shape
    logcum = jnp.cumsum(-decay_rate, axis=1).reshape(S, -1, BLK)
    pay = (S // 2) * SK + 8
    vmem = pl.BlockSpec(memory_space=pltpu.VMEM)
    dma = pltpu.SemaphoreType.DMA
    f32, bf16 = jnp.float32, jnp.bfloat16
    return pl.pallas_call(
        functools.partial(kernel, nq, nk),
        out_shape=(
            jax.ShapeDtypeStruct((S, SK, D), f32),
            jax.ShapeDtypeStruct((S, SK, D), f32),
            jax.ShapeDtypeStruct((S, SK), f32),
        ),
        in_specs=[vmem] * 5 + [pl.BlockSpec(memory_space=pltpu.SMEM)],
        out_specs=(vmem, vmem, vmem),
        scratch_shapes=[
            pltpu.VMEM((SLOTS, S, 2, SK, D), bf16),
            pltpu.VMEM((SLOTS, S, 2, SK, D), bf16),
            pltpu.VMEM((SLOTS, S, BLK, R), f32),
            pltpu.VMEM((SLOTS, S, 1, R), f32),
            pltpu.VMEM((SLOTS, S, 1, R), f32),
            pltpu.VMEM((SLOTS, S, 1, R), f32),
            pltpu.VMEM((SLOTS, S, BLK, BLK), f32),
            pltpu.VMEM((S, D, R), f32),
            pltpu.VMEM((S, 8, R), f32),
            pltpu.VMEM((SLOTS, 2, 2, pay, D), f32),
            pltpu.VMEM((SLOTS, 2, pay, D), f32),
            pltpu.VMEM((3, 2, pay, D), f32),
            pltpu.VMEM((3, 2, pay, D), f32),
            pltpu.VMEM((nk, 2, pay, D), f32),
            pltpu.VMEM((nk, 2, pay, D), f32),
            pltpu.VMEM((2, S, 1, R), f32),
            pltpu.VMEM((nk, 2, S, 1, R), f32),
        ]
        + [dma((SLOTS,))] * 8
        + [dma((nk,))] * 2
        + [dma((SLOTS, 2))] * 2
        + [dma((3, 2))] * 4
        + [dma((nk, 2))] * 2,
        compiler_params=pltpu.CompilerParams(
            collective_id=0, has_side_effects=True, vmem_limit_bytes=48 * 1024 * 1024
        ),
    )(queries, c_proj, keys, b_proj, logcum, doc_ids)


def solution(mesh):
    placed = (
        P(None, "qb", None),
        P(None, ("qb", "kb"), None),
        P(None, "qb", None),
        P(None, ("qb", "kb"), None),
        P(),
        P(),
    )
    return jax.shard_map(
        functools.partial(shards, mesh.shape["qb"], mesh.shape["kb"]),
        mesh=mesh,
        in_specs=placed,
        out_specs=(P(None, ("qb", "kb"), None), P(None, ("qb", "kb"), None), P(None, ("qb", "kb"))),
        check_vma=False,
    )
```

```python
import functools
import math

import jax
import jax.numpy as jnp
from jax import lax
from jax.experimental import pallas as pl
from jax.experimental.pallas import tpu as pltpu
from jax.sharding import PartitionSpec as P

MESH = pl.DeviceIdType.MESH
HIGHEST = lax.Precision.HIGHEST
NEG = -1e30
SK = 64
BLK = 128
SLOTS = 7
WAVES = 2


def nt(a, b, precision=None):
    return lax.dot_general(
        a, b, (((1,), (1,)), ((), ())), preferred_element_type=jnp.float32, precision=precision
    )


def kernel(
    nq, nk,
    q_ref, c_ref, k_ref, b_ref, rate_ref, doc_ref,
    gc_ref, gb_ref, gl_ref,
    qbuf, cbuf, kbuf, bbuf, ebuf, mbuf, lbuf, fbuf, lcs, lckb, gct, rf, gp, up, dn, gcp, gcr, st, str_, fin, got, held,
    ks, kr, bs, br, qs, qr, cs, cr, hs, hr, sts, strs, us, ur, ds, dr, gcs, gcrs, fs, fr,
):
    S, R, D = q_ref.shape
    RB = R // BLK
    NB = nq * RB
    RR = 2 * R
    nx = nk // 2
    npair = nq // 2
    qb = lax.axis_index("qb")
    kb = lax.axis_index("kb")
    pr = qb // 2
    core = qb % 2
    other = 1 - core
    kx = kb // 2
    ky = kb % 2
    both = range(2)
    me = 2 * ky + core

    def side(g):
        return ky if g == 0 else 1 - ky

    def dev(step, which, g=0):
        return (((pr + step + npair) % npair) * 2 + which, kx * 2 + side(g))

    sibling = dev(0, other)
    crowd = [(dx, g) for dx in range(nx) for g in both if dx or g]

    def peer(dx, g):
        return (qb, ((kx + dx) % nx) * 2 + side(g))

    barrier = pltpu.get_barrier_semaphore()
    partners = [dev(step, u, g) for step in (1, -1, 6, -6) for u in both for g in both]
    partners += [sibling, dev(0, other, 1)] + [peer(dx, g) for dx, g in crowd]
    for to in partners:
        pl.semaphore_signal(barrier, inc=1, device_id=to, device_id_type=MESH)

    def rc(src, dst, ssem, rsem, to):
        return pltpu.make_async_remote_copy(
            src_ref=src, dst_ref=dst, send_sem=ssem, recv_sem=rsem, device_id=to, device_id_type=MESH
        )

    def own_push(own, buf, ssem, rsem):
        push, land = {}, {}
        for e in (0, 1, 6):
            for g in both:
                push[e, g], land[e, g] = [], []
                for v in both:
                    if e == g == v == 0:
                        continue
                    which = (core + v) % 2
                    push[e, g].append(rc(
                        own.at[2 * side(g) + which], buf.at[e, g, core],
                        ssem.at[e, g, v], rsem.at[e, g, v], dev(e, which, g),
                    ))
                    land[e, g].append(rc(
                        buf.at[e, g, which], buf.at[e, g, which],
                        ssem.at[e, g, v], rsem.at[e, g, v], dev(-e, which, g),
                    ))
        return push, land

    def pass_on(buf, ssem, rsem):
        out = {}
        for e, f, step in ((2, 1, 1), (3, 2, 1), (5, 6, -1), (4, 5, -1)):
            for g in both:
                out[e, g] = rc(
                    buf.at[f, g], buf.at[e, g], ssem.at[e, g, 0], rsem.at[e, g, 0], dev(step, core)
                )
        return out

    def swap(own, buf, ssem, rsem):
        return (
            rc(own.at[2 * ky + other], buf.at[core], ssem, rsem, sibling),
            rc(buf.at[other], buf.at[other], ssem, rsem, sibling),
        )

    kp, kl = own_push(k_ref, kbuf, ks, kr)
    bp, bl = own_push(b_ref, bbuf, bs, br)
    kf, bf = pass_on(kbuf, ks, kr), pass_on(bbuf, bs, br)
    qx = swap(q_ref, qbuf, qs, qr)
    cx = swap(c_ref, cbuf, cs, cr)

    lane = lax.broadcasted_iota(jnp.int32, (1, BLK), 1)
    sub = lax.broadcasted_iota(jnp.int32, (BLK, BLK), 0)

    def key_block(e, g, u):
        j = (pr - e + npair) % npair
        return (2 * j + u) * RB + ((kx * 2 + side(g)) * SK) // BLK

    def key_columns(e, w):
        first = lcs[pl.ds(key_block(e, w, 0), 1), :]
        second = lcs[pl.ds(key_block(e, w, 1), 1), :]
        low = jnp.concatenate([first[:, :SK], second[:, :SK]], axis=1)
        high = jnp.concatenate([first[:, SK:], second[:, SK:]], axis=1)
        row = jnp.where(jnp.full((1, BLK), side(w)) == 0, low, high)
        lckb[e, w] = jnp.broadcast_to(row, (BLK, BLK)).T

    kbuf[0, 0, core] = k_ref[me]
    bbuf[0, 0, core] = b_ref[me]
    pl.semaphore_wait(barrier, len(partners))

    def push(copies, e, w):
        for copy in copies[e, w]:
            copy.start()

    for g in both:
        push(kp, 6, g)
    for g in both:
        push(kp, 1, g)
    for g in both:
        push(kp, 0, g)
    qx[0].start()
    for g in both:
        push(bp, 6, g)
    for g in both:
        push(bp, 1, g)
    for g in both:
        push(bp, 0, g)
    cx[0].start()

    rates = rate_ref[me]
    row = lax.broadcasted_iota(jnp.int32, (BLK, BLK), 0)
    col = lax.broadcasted_iota(jnp.int32, (BLK, BLK), 1)
    within = jnp.dot(
        rates, (row <= col).astype(jnp.float32), preferred_element_type=jnp.float32, precision=HIGHEST
    )
    row = lax.broadcasted_iota(jnp.int32, (NB, NB), 0)
    col = lax.broadcasted_iota(jnp.int32, (NB, NB), 1)
    base = pr * 2 * RB
    after = ((col >= base) & (col < row)).astype(jnp.float32)
    before = ((col >= row) & (col < base)).astype(jnp.float32)
    blocks = jnp.dot(
        after - before, rates, preferred_element_type=jnp.float32, precision=HIGHEST
    )
    lcs[...] = -(within + jnp.sum(blocks, axis=1, keepdims=True))

    for e in range(SLOTS):
        for w in range(WAVES):
            key_columns(e, w)

    qbuf[core] = q_ref[me]
    cbuf[core] = c_ref[me]
    gct[...] = jnp.zeros_like(gct)
    rf[...] = jnp.zeros_like(rf)
    gp[:, :, BLK:, :] = jnp.zeros((SLOTS, WAVES, 8, D), jnp.float32)
    gcp[:, BLK:, :] = jnp.zeros((nk, 8, D), jnp.float32)
    fin[:, :, BLK:, :] = jnp.zeros((WAVES, 2, 8, D), jnp.float32)

    def biases(e, w, r):
        rd = doc_ref[me, pr * 2 * RB + r]
        out = []
        for u in range(2):
            same = doc_ref[me, key_block(e, w, u)] == rd
            if e:
                same = same & (pr >= e)
            out.append(jnp.where(same, 0.0, NEG).astype(jnp.float32))
        return out

    def causal(w, r):
        kpos = (2 * pr) * R + (kx * 2 + side(w)) * SK + jnp.where(sub >= SK, sub - SK + R, sub)
        rpos = pr * RR + r * BLK + lane
        return kpos <= rpos

    scale = (D ** -0.5) * math.log2(math.e)

    def first_pass(e, w):
        every = nt(kbuf[e, w].reshape(BLK, D), qbuf[...].reshape(RR, D)) * scale
        for r in range(2 * RB):
            cols = slice(r * BLK, (r + 1) * BLK)
            sc = every[:, cols]
            if e == 0:
                sc = jnp.where(causal(w, r), sc, NEG)
            bias = biases(e, w, r)
            halves = [sc[:SK], sc[SK:]]
            top = jnp.maximum(
                jnp.max(halves[0], axis=0, keepdims=True) + bias[0],
                jnp.max(halves[1], axis=0, keepdims=True) + bias[1],
            )
            total = jnp.zeros((1, BLK), jnp.float32)
            for u in range(2):
                ex = jnp.exp2(halves[u] - jnp.maximum(top, NEG - 2.0 * bias[u]))
                ebuf[e, w, u * SK:(u + 1) * SK, cols] = ex
                total += jnp.sum(ex, axis=0, keepdims=True)
            mbuf[e, w, :, cols] = top
            lbuf[e, w, :, cols] = total

    def passed(w, *slots):
        for land, forward in ((kl, kf), (bl, bf)):
            for e in slots:
                if e in (0, 1, 6):
                    for copy in land[e, w]:
                        copy.wait_recv()
                else:
                    forward[e, w].wait_recv()
                follow = {1: 2, 2: 3, 6: 5, 5: 4}.get(e)
                if follow is not None:
                    forward[follow, w].start()

    stats = [rc(st, str_.at[o], sts.at[o], strs.at[o], peer(o, 0)) for o in range(1, nx)]
    every = [(e, w) for e in range(SLOTS) for w in both]

    for w in both:
        for copy in kl[0, w]:
            copy.wait_recv()
    qx[1].wait_recv()
    for w in both:
        first_pass(0, w)
    for w in both:
        passed(w, 1, 6)
        first_pass(1, w)
        first_pass(6, w)
    for w in both:
        passed(w, 2, 5)
        first_pass(2, w)
        first_pass(5, w)
    for w in both:
        kf[3, w].wait_recv()
        kf[4, w].wait_recv()
        first_pass(3, w)
        first_pass(4, w)
    top = mbuf[0, 0]
    for at in every:
        top = jnp.maximum(top, mbuf[at])
    total = jnp.zeros_like(top)
    for at in every:
        total += lbuf[at] * jnp.exp2(mbuf[at] - top)
    st[0] = top
    st[1] = total
    for copy in stats:
        copy.start()
    for w in both:
        for copy in bl[0, w]:
            copy.wait_recv()
        for e in (3, 4):
            bf[e, w].wait_recv()
    cx[1].wait_recv()
    for copy in stats:
        copy.wait_recv()
    best = top
    for o in range(1, nx):
        best = jnp.maximum(best, str_[o, 0])
    whole = total * jnp.exp2(top - best)
    for o in range(1, nx):
        whole += str_[o, 1] * jnp.exp2(str_[o, 0] - best)
    for at in every:
        fbuf[at] = jnp.exp2(mbuf[at] - best) / whole

    ones = jnp.ones((8, BLK), jnp.float32)

    def second_pass(e, w):
        bb = bbuf[e, w].reshape(BLK, D)
        bt = bb.T
        kcol = lckb[e, w]
        crows = cbuf[...].reshape(RR, D)
        products = nt(bb, crows)
        weights = []
        gathered = jnp.zeros((BLK, BLK), jnp.float32)
        for r in range(2 * RB):
            cols = slice(r * BLK, (r + 1) * BLK)
            bias = biases(e, w, r)
            rows = lcs[pl.ds(pr * 2 * RB + r, 1), :]
            spread = jnp.concatenate(
                [(rows + bias[0]) - kcol[:SK], (rows + bias[1]) - kcol[SK:]], axis=0
            )
            if e == 0:
                spread = jnp.where(causal(w, r), spread, NEG)
            decay = jnp.exp(spread)
            mixing = products[:, cols] * decay
            gap = mixing - ebuf[e, w, :, cols] * fbuf[e, w, :, cols]
            flow = gap * mixing
            weights.append((gap * decay).astype(jnp.bfloat16))
            gathered += flow
            rf[:, cols] += jnp.sum(flow.reshape(BLK // 8, 8, BLK), axis=0)
        wide = jnp.concatenate(weights, axis=1)
        gct[...] += jnp.dot(bt, wide, preferred_element_type=jnp.float32)
        gp[e, w, :BLK, :] = jnp.dot(wide, crows, preferred_element_type=jnp.float32)
        gp[e, w, BLK:BLK + 1, :] = nt(ones, gathered, HIGHEST)[0:1]

    uc = [
        [
            rc(gp.at[e, w], up.at[i, w], us.at[i, w], ur.at[i, w], dev(-1, core, w if e == 1 else 0))
            for w in both
        ]
        for i, e in enumerate((3, 2, 1))
    ]
    dc = [
        [
            rc(
                gp.at[e, w], dn.at[i, w], ds.at[i, w], dr.at[i, w],
                dev(-6, core, w) if e == 6 else dev(1, core),
            )
            for w in both
        ]
        for i, e in enumerate((4, 5, 6))
    ]
    cc = {
        (dx, g): rc(
            gcp.at[((kx + dx) % nx) * 2 + side(g)], gcr.at[dx, g],
            gcs.at[dx, g], gcrs.at[dx, g], peer(dx, g),
        )
        for dx, g in crowd
    }
    fx = [rc(fin.at[w, other], got.at[w], fs.at[w], fr.at[w], sibling) for w in both]
    hx = rc(gp.at[0, 1], held, hs, hr, dev(0, core, 1))

    def chain(w, step):
        for e, copies, landed in ((4 + step, dc, dn), (3 - step, uc, up)):
            if step:
                copies[step - 1][w].wait_recv()
                gp[e, w] = gp[e, w] + landed[step - 1, w]
            copies[step][w].start()

    def finish(w):
        uc[2][w].wait_recv()
        dc[2][w].wait_recv()
        if w:
            hx.wait_recv()
            bsum = held[...]
        else:
            bsum = gp[0, 0]
        bsum = (bsum + (up[2, w] + dn[2, w])) * 2.0
        for dx in range(nx):
            if dx or w:
                cc[dx, w].wait_recv()
        csum = gcr[0, 1] if w else gcp[kb]
        for dx in range(1, nx):
            csum += gcr[dx, w]
        csum = csum * 2.0
        flows = []
        for u in range(2):
            fin[w, u, :SK, :] = bsum[u * SK:(u + 1) * SK]
            fin[w, u, SK:BLK, :] = csum[u * SK:(u + 1) * SK]
            rowf = csum[BLK + u:BLK + u + 1]
            rowf = jnp.where(jnp.full((1, SK), ky) == 0, rowf[:, :SK], rowf[:, SK:])
            flows.append(rowf - bsum[BLK:BLK + 1, u * SK:(u + 1) * SK])
        flows = jnp.concatenate(flows, axis=1)
        for u in range(2):
            fin[w, u, BLK:BLK + 1, :] = flows
        fx[w].start()
        gb_ref[2 * side(w) + core] = fin[w, core, :SK, :]
        gc_ref[2 * side(w) + core] = fin[w, core, SK:BLK, :]

    for w in both:
        second_pass(3, w)
        second_pass(4, w)
        chain(w, 0)
    for w in both:
        second_pass(2, w)
        second_pass(5, w)
    for w in both:
        second_pass(1, w)
        second_pass(6, w)
        chain(w, 1)
    second_pass(0, 1)
    hx.start()
    second_pass(0, 0)
    turned = gct[...].T
    flows = jnp.sum(rf[...], axis=0, keepdims=True)
    for o in range(nk):
        for u in range(2):
            at = u * R + o * SK
            gcp[o, u * SK:(u + 1) * SK, :] = turned[at:at + SK]
            at = u * R + (o * SK) // BLK * BLK
            gcp[o, BLK + u:BLK + u + 1, :] = flows[:, at:at + BLK]
    for at in sorted(cc, key=lambda at: -at[1]):
        cc[at].start()
    chain(0, 2)
    chain(1, 2)
    finish(0)
    finish(1)

    for w in both:
        fx[w].wait_recv()
        gb_ref[2 * side(w) + other] = got[w, :SK, :]
        gc_ref[2 * side(w) + other] = got[w, SK:BLK, :]

    def pick(flag, a, b):
        return jnp.where(jnp.full((1, BLK), flag) == 0, a, b)

    ours = [fin[w, core, BLK:BLK + 1, :] for w in both]
    rest = [got[w, BLK:BLK + 1, :] for w in both]
    ours = [pick(ky, ours[0], ours[1]), pick(ky, ours[1], ours[0])]
    rest = [pick(ky, rest[0], rest[1]), pick(ky, rest[1], rest[0])]
    flows = jnp.concatenate(
        [pick(core, x, y) for y_hi in both for x, y in ((ours[y_hi], rest[y_hi]), (rest[y_hi], ours[y_hi]))],
        axis=0,
    )
    gl_ref[...] = jnp.where(jnp.full((S, SK), core) == 0, flows[:, :SK], flows[:, SK:])

    for copies in list(kp.values()) + list(bp.values()) + uc + dc:
        for copy in copies:
            copy.wait_send()
    for copy in list(kf.values()) + list(bf.values()) + stats + list(cc.values()) + fx:
        copy.wait_send()
    for copy in (qx[0], cx[0], hx):
        copy.wait_send()


def shards(nq, nk, queries, keys, c_proj, b_proj, decay_rate, doc_ids):
    S, R, D = queries.shape
    rates = decay_rate.reshape(S, -1, BLK)
    NB = rates.shape[1]
    RR = 2 * R
    pay = BLK + 8
    vmem = pl.BlockSpec(memory_space=pltpu.VMEM)
    dma = pltpu.SemaphoreType.DMA
    f32, bf16 = jnp.float32, jnp.bfloat16
    return pl.pallas_call(
        functools.partial(kernel, nq, nk),
        out_shape=(
            jax.ShapeDtypeStruct((S, SK, D), f32),
            jax.ShapeDtypeStruct((S, SK, D), f32),
            jax.ShapeDtypeStruct((S, SK), f32),
        ),
        in_specs=[vmem] * 5 + [pl.BlockSpec(memory_space=pltpu.SMEM)],
        out_specs=(vmem, vmem, vmem),
        scratch_shapes=[
            pltpu.VMEM((2, R, D), bf16),
            pltpu.VMEM((2, R, D), bf16),
            pltpu.VMEM((SLOTS, WAVES, 2, SK, D), bf16),
            pltpu.VMEM((SLOTS, WAVES, 2, SK, D), bf16),
            pltpu.VMEM((SLOTS, WAVES, BLK, RR), f32),
            pltpu.VMEM((SLOTS, WAVES, 1, RR), f32),
            pltpu.VMEM((SLOTS, WAVES, 1, RR), f32),
            pltpu.VMEM((SLOTS, WAVES, 1, RR), f32),
            pltpu.VMEM((NB, BLK), f32),
            pltpu.VMEM((SLOTS, WAVES, BLK, BLK), f32),
            pltpu.VMEM((D, RR), f32),
            pltpu.VMEM((8, RR), f32),
            pltpu.VMEM((SLOTS, WAVES, pay, D), f32),
            pltpu.VMEM((3, WAVES, pay, D), f32),
            pltpu.VMEM((3, WAVES, pay, D), f32),
            pltpu.VMEM((nk, pay, D), f32),
            pltpu.VMEM((nk // 2, 2, pay, D), f32),
            pltpu.VMEM((2, 1, RR), f32),
            pltpu.VMEM((nk // 2, 2, 1, RR), f32),
            pltpu.VMEM((WAVES, 2, pay, D), f32),
            pltpu.VMEM((WAVES, pay, D), f32),
            pltpu.VMEM((pay, D), f32),
        ]
        + [dma((SLOTS, WAVES, 2))] * 4
        + [dma] * 6
        + [dma((nk // 2,))] * 2
        + [dma((3, WAVES))] * 4
        + [dma((nk // 2, 2))] * 2
        + [dma((WAVES,))] * 2,
        compiler_params=pltpu.CompilerParams(
            collective_id=0, has_side_effects=True, vmem_limit_bytes=48 * 1024 * 1024
        ),
    )(queries, c_proj, keys, b_proj, rates, doc_ids)


def solution(mesh):
    placed = (
        P(None, "qb", None),
        P(None, ("qb", "kb"), None),
        P(None, "qb", None),
        P(None, ("qb", "kb"), None),
        P(),
        P(),
    )
    return jax.shard_map(
        functools.partial(shards, mesh.shape["qb"], mesh.shape["kb"]),
        mesh=mesh,
        in_specs=placed,
        out_specs=(P(None, ("qb", "kb"), None), P(None, ("qb", "kb"), None), P(None, ("qb", "kb"))),
        check_vma=False,
    )
```

```python
import functools
import math

import jax
import jax.numpy as jnp
from jax import lax
from jax.experimental import pallas as pl
from jax.experimental.pallas import tpu as pltpu
from jax.sharding import PartitionSpec as P

MESH = pl.DeviceIdType.MESH
HIGHEST = lax.Precision.HIGHEST
NEG = -1e30
SK = 64
BLK = 128
SLOTS = 7
WAVES = 2


def nt(a, b, precision=None):
    return lax.dot_general(
        a, b, (((1,), (1,)), ((), ())), preferred_element_type=jnp.float32, precision=precision
    )


def kernel(
    nq, nk,
    q_ref, c_ref, k_ref, b_ref, rate_ref, doc_ref,
    gc_ref, gb_ref, gl_ref,
    qbuf, cbuf, kbuf, bbuf, ebuf, mbuf, lbuf, fbuf, lcs, lckb, gct, rf, gp, up, dn, gcp, gcr, st, str_, fin, got, held, rbuf, mixbuf, decbuf,
    ls, ks, kr, bs, br, qs, qr, cs, cr, hs, hr, sts, strs, us, ur, ds, dr, gcs, gcrs, fs, fr,
):
    S, R, D = q_ref.shape
    RB = R // BLK
    NB = nq * RB
    RR = 2 * R
    nx = nk // 2
    npair = nq // 2
    qb = lax.axis_index("qb")
    kb = lax.axis_index("kb")
    pr = qb // 2
    core = qb % 2
    other = 1 - core
    kx = kb // 2
    ky = kb % 2
    both = range(2)
    me = 2 * ky + core

    def side(g):
        return ky if g == 0 else 1 - ky

    def dev(step, which, g=0):
        return (((pr + step + npair) % npair) * 2 + which, kx * 2 + side(g))

    sibling = dev(0, other)
    crowd = [(dx, g) for dx in range(nx) for g in both if dx or g]

    def peer(dx, g):
        return (qb, ((kx + dx) % nx) * 2 + side(g))

    barrier = pltpu.get_barrier_semaphore()
    partners = [dev(step, u, g) for step in (1, -1, 6, -6) for u in both for g in both]
    partners += [sibling, dev(0, other, 1)] + [peer(dx, g) for dx, g in crowd]
    for to in partners:
        pl.semaphore_signal(barrier, inc=1, device_id=to, device_id_type=MESH)

    def rc(src, dst, ssem, rsem, to):
        return pltpu.make_async_remote_copy(
            src_ref=src, dst_ref=dst, send_sem=ssem, recv_sem=rsem, device_id=to, device_id_type=MESH
        )

    def own_push(own, buf, ssem, rsem):
        push, land = {}, {}
        for e in (0, 1, 6):
            for g in both:
                push[e, g], land[e, g] = [], []
                for v in both:
                    if e == g == v == 0:
                        continue
                    which = (core + v) % 2
                    push[e, g].append(rc(
                        own.at[2 * side(g) + which], buf.at[e, g, core],
                        ssem.at[e, g, v], rsem.at[e, g, v], dev(e, which, g),
                    ))
                    land[e, g].append(rc(
                        buf.at[e, g, which], buf.at[e, g, which],
                        ssem.at[e, g, v], rsem.at[e, g, v], dev(-e, which, g),
                    ))
        return push, land

    def pass_on(buf, ssem, rsem):
        out = {}
        for e, f, step in ((2, 1, 1), (3, 2, 1), (5, 6, -1), (4, 5, -1)):
            for g in both:
                out[e, g] = rc(
                    buf.at[f, g], buf.at[e, g], ssem.at[e, g, 0], rsem.at[e, g, 0], dev(step, core)
                )
        return out

    def swap(own, buf, ssem, rsem):
        return (
            rc(own.at[2 * ky + other], buf.at[core], ssem, rsem, sibling),
            rc(buf.at[other], buf.at[other], ssem, rsem, sibling),
        )

    kp, kl = own_push(k_ref, kbuf, ks, kr)
    bp, bl = own_push(b_ref, bbuf, bs, br)
    kf, bf = pass_on(kbuf, ks, kr), pass_on(bbuf, bs, br)
    qx = swap(q_ref, qbuf, qs, qr)
    cx = swap(c_ref, cbuf, cs, cr)

    local = [
        pltpu.make_async_copy(src, dst, ls.at[i])
        for i, (src, dst) in enumerate((
            (k_ref.at[me], kbuf.at[0, 0, core]),
            (q_ref.at[me], qbuf.at[core]),
            (rate_ref, rbuf),
            (b_ref.at[me], bbuf.at[0, 0, core]),
            (c_ref.at[me], cbuf.at[core]),
        ))
    ]
    for copy in local:
        copy.start()

    lane = lax.broadcasted_iota(jnp.int32, (1, BLK), 1)
    sub = lax.broadcasted_iota(jnp.int32, (BLK, BLK), 0)

    def key_block(e, g, u):
        j = (pr - e + npair) % npair
        return (2 * j + u) * RB + ((kx * 2 + side(g)) * SK) // BLK

    def key_columns(e, w):
        first = lcs[pl.ds(key_block(e, w, 0), 1), :]
        second = lcs[pl.ds(key_block(e, w, 1), 1), :]
        low = jnp.concatenate([first[:, :SK], second[:, :SK]], axis=1)
        high = jnp.concatenate([first[:, SK:], second[:, SK:]], axis=1)
        row = jnp.where(jnp.full((1, BLK), side(w)) == 0, low, high)
        lckb[e, w] = jnp.broadcast_to(row, (BLK, BLK)).T

    pl.semaphore_wait(barrier, len(partners))

    def push(copies, e, w):
        for copy in copies[e, w]:
            copy.start()

    for g in both:
        push(kp, 6, g)
    for g in both:
        push(kp, 1, g)
    for g in both:
        push(kp, 0, g)
    qx[0].start()
    for g in both:
        push(bp, 6, g)
    for g in both:
        push(bp, 1, g)
    for g in both:
        push(bp, 0, g)
    cx[0].start()

    local[2].wait()
    row = lax.broadcasted_iota(jnp.int32, (NB, NB * S), 0)
    col = lax.broadcasted_iota(jnp.int32, (NB, NB * S), 1)
    ours = (col % S) == me
    blk = col // S
    base = pr * 2 * RB
    rates = jnp.dot(
        (ours & (blk == row)).astype(jnp.float32), rbuf[...],
        preferred_element_type=jnp.float32, precision=HIGHEST,
    )
    after = (ours & (blk >= base) & (blk < row)).astype(jnp.float32)
    before = (ours & (blk >= row) & (blk < base)).astype(jnp.float32)
    blocks = jnp.dot(
        after - before, rbuf[...], preferred_element_type=jnp.float32, precision=HIGHEST
    )
    row = lax.broadcasted_iota(jnp.int32, (BLK, BLK), 0)
    col = lax.broadcasted_iota(jnp.int32, (BLK, BLK), 1)
    within = jnp.dot(
        rates, (row <= col).astype(jnp.float32), preferred_element_type=jnp.float32, precision=HIGHEST
    )
    lcs[...] = -(within + jnp.sum(blocks, axis=1, keepdims=True))

    for e in range(SLOTS):
        for w in range(WAVES):
            key_columns(e, w)

    gct[...] = jnp.zeros_like(gct)
    rf[...] = jnp.zeros_like(rf)
    gp[:, :, BLK:, :] = jnp.zeros((SLOTS, WAVES, 8, D), jnp.float32)
    gcp[:, BLK:, :] = jnp.zeros((nk, 8, D), jnp.float32)
    fin[:, :, BLK:, :] = jnp.zeros((WAVES, 2, 8, D), jnp.float32)

    def biases(e, w, r):
        rd = doc_ref[me, pr * 2 * RB + r]
        out = []
        for u in range(2):
            same = doc_ref[me, key_block(e, w, u)] == rd
            if e:
                same = same & (pr >= e)
            out.append(jnp.where(same, 0.0, NEG).astype(jnp.float32))
        return out

    def causal(w, r):
        kpos = (2 * pr) * R + (kx * 2 + side(w)) * SK + jnp.where(sub >= SK, sub - SK + R, sub)
        rpos = pr * RR + r * BLK + lane
        return kpos <= rpos

    scale = (D ** -0.5) * math.log2(math.e)

    def first_pass(e, w):
        every = nt(kbuf[e, w].reshape(BLK, D), qbuf[...].reshape(RR, D)) * scale
        for r in range(2 * RB):
            cols = slice(r * BLK, (r + 1) * BLK)
            sc = every[:, cols]
            if e == 0:
                sc = jnp.where(causal(w, r), sc, NEG)
            bias = biases(e, w, r)
            halves = [sc[:SK], sc[SK:]]
            top = jnp.maximum(
                jnp.max(halves[0], axis=0, keepdims=True) + bias[0],
                jnp.max(halves[1], axis=0, keepdims=True) + bias[1],
            )
            total = jnp.zeros((1, BLK), jnp.float32)
            for u in range(2):
                ex = jnp.exp2(halves[u] - jnp.maximum(top, NEG - 2.0 * bias[u]))
                ebuf[e, w, u * SK:(u + 1) * SK, cols] = ex
                total += jnp.sum(ex, axis=0, keepdims=True)
            mbuf[e, w, :, cols] = top
            lbuf[e, w, :, cols] = total

    def mix_pass(e, w):
        kcol = lckb[e, w]
        products = nt(bbuf[e, w].reshape(BLK, D), cbuf[...].reshape(RR, D))
        for r in range(2 * RB):
            cols = slice(r * BLK, (r + 1) * BLK)
            bias = biases(e, w, r)
            rows = lcs[pl.ds(pr * 2 * RB + r, 1), :]
            spread = jnp.concatenate(
                [(rows + bias[0]) - kcol[:SK], (rows + bias[1]) - kcol[SK:]], axis=0
            )
            if e == 0:
                spread = jnp.where(causal(w, r), spread, NEG)
            decay = jnp.exp(spread)
            decbuf[e, w, :, cols] = decay
            mixbuf[e, w, :, cols] = products[:, cols] * decay

    def passed(w, *slots):
        for land, forward in ((kl, kf), (bl, bf)):
            for e in slots:
                if e in (0, 1, 6):
                    for copy in land[e, w]:
                        copy.wait_recv()
                else:
                    forward[e, w].wait_recv()
                follow = {1: 2, 2: 3, 6: 5, 5: 4}.get(e)
                if follow is not None:
                    forward[follow, w].start()

    stats = [rc(st, str_.at[o], sts.at[o], strs.at[o], peer(o, 0)) for o in range(1, nx)]
    every = [(e, w) for e in range(SLOTS) for w in both]

    for w in both:
        for copy in kl[0, w]:
            copy.wait_recv()
    qx[1].wait_recv()
    local[0].wait()
    local[1].wait()
    for w in both:
        first_pass(0, w)
    for w in both:
        passed(w, 1, 6)
    for w in both:
        first_pass(1, w)
        first_pass(6, w)
    for w in both:
        for copy in bl[0, w]:
            copy.wait_recv()
    cx[1].wait_recv()
    local[3].wait()
    local[4].wait()
    mix_pass(0, 0)
    mix_pass(0, 1)
    for w in both:
        passed(w, 2, 5)
    for w in both:
        first_pass(2, w)
        first_pass(5, w)
    for w in both:
        mix_pass(1, w)
        mix_pass(6, w)
    for w in both:
        kf[3, w].wait_recv()
        kf[4, w].wait_recv()
        first_pass(3, w)
        first_pass(4, w)
    top = mbuf[0, 0]
    for at in every:
        top = jnp.maximum(top, mbuf[at])
    total = jnp.zeros_like(top)
    for at in every:
        total += lbuf[at] * jnp.exp2(mbuf[at] - top)
    st[0] = top
    st[1] = total
    for copy in stats:
        copy.start()
    for w in both:
        for e in (3, 4):
            bf[e, w].wait_recv()
            mix_pass(e, w)
    for w in both:
        mix_pass(2, w)
        mix_pass(5, w)
    for copy in stats:
        copy.wait_recv()
    best = top
    for o in range(1, nx):
        best = jnp.maximum(best, str_[o, 0])
    whole = total * jnp.exp2(top - best)
    for o in range(1, nx):
        whole += str_[o, 1] * jnp.exp2(str_[o, 0] - best)
    for at in every:
        fbuf[at] = jnp.exp2(mbuf[at] - best) / whole

    ones = jnp.ones((8, BLK), jnp.float32)

    def second_pass(e, w):
        bt = bbuf[e, w].reshape(BLK, D).T
        weights = []
        gathered = jnp.zeros((BLK, BLK), jnp.float32)
        for r in range(2 * RB):
            cols = slice(r * BLK, (r + 1) * BLK)
            mixing = mixbuf[e, w, :, cols]
            gap = mixing - ebuf[e, w, :, cols] * fbuf[e, w, :, cols]
            flow = gap * mixing
            weights.append((gap * decbuf[e, w, :, cols]).astype(jnp.bfloat16))
            gathered += flow
            rf[:, cols] += jnp.sum(flow.reshape(BLK // 8, 8, BLK), axis=0)
        wide = jnp.concatenate(weights, axis=1)
        gct[...] += jnp.dot(bt, wide, preferred_element_type=jnp.float32)
        gp[e, w, :BLK, :] = jnp.dot(wide, cbuf[...].reshape(RR, D), preferred_element_type=jnp.float32)
        gp[e, w, BLK:BLK + 1, :] = nt(ones, gathered, HIGHEST)[0:1]

    uc = [
        [
            rc(gp.at[e, w], up.at[i, w], us.at[i, w], ur.at[i, w], dev(-1, core, w if e == 1 else 0))
            for w in both
        ]
        for i, e in enumerate((3, 2, 1))
    ]
    dc = [
        [
            rc(
                gp.at[e, w], dn.at[i, w], ds.at[i, w], dr.at[i, w],
                dev(-6, core, w) if e == 6 else dev(1, core),
            )
            for w in both
        ]
        for i, e in enumerate((4, 5, 6))
    ]
    cc = {
        (dx, g): rc(
            gcp.at[((kx + dx) % nx) * 2 + side(g)], gcr.at[dx, g],
            gcs.at[dx, g], gcrs.at[dx, g], peer(dx, g),
        )
        for dx, g in crowd
    }
    fx = [rc(fin.at[w, other], got.at[w], fs.at[w], fr.at[w], sibling) for w in both]
    hx = rc(gp.at[0, 1], held, hs, hr, dev(0, core, 1))

    def chain(w, step):
        for e, copies, landed in ((4 + step, dc, dn), (3 - step, uc, up)):
            if step:
                copies[step - 1][w].wait_recv()
                gp[e, w] = gp[e, w] + landed[step - 1, w]
            copies[step][w].start()

    def finish(w):
        uc[2][w].wait_recv()
        dc[2][w].wait_recv()
        if w:
            hx.wait_recv()
            bsum = held[...]
        else:
            bsum = gp[0, 0]
        bsum = (bsum + (up[2, w] + dn[2, w])) * 2.0
        for dx in range(nx):
            if dx or w:
                cc[dx, w].wait_recv()
        csum = gcr[0, 1] if w else gcp[kb]
        for dx in range(1, nx):
            csum += gcr[dx, w]
        csum = csum * 2.0
        flows = []
        for u in range(2):
            fin[w, u, :SK, :] = bsum[u * SK:(u + 1) * SK]
            fin[w, u, SK:BLK, :] = csum[u * SK:(u + 1) * SK]
            rowf = csum[BLK + u:BLK + u + 1]
            rowf = jnp.where(jnp.full((1, SK), ky) == 0, rowf[:, :SK], rowf[:, SK:])
            flows.append(rowf - bsum[BLK:BLK + 1, u * SK:(u + 1) * SK])
        flows = jnp.concatenate(flows, axis=1)
        for u in range(2):
            fin[w, u, BLK:BLK + 1, :] = flows
        fx[w].start()
        gb_ref[2 * side(w) + core] = fin[w, core, :SK, :]
        gc_ref[2 * side(w) + core] = fin[w, core, SK:BLK, :]

    for w in both:
        second_pass(3, w)
        second_pass(4, w)
        chain(w, 0)
    for w in both:
        second_pass(2, w)
        second_pass(5, w)
    for w in both:
        second_pass(1, w)
        second_pass(6, w)
        chain(w, 1)
    second_pass(0, 1)
    hx.start()
    second_pass(0, 0)
    turned = gct[...].T
    flows = jnp.sum(rf[...], axis=0, keepdims=True)
    for o in range(nk):
        for u in range(2):
            at = u * R + o * SK
            gcp[o, u * SK:(u + 1) * SK, :] = turned[at:at + SK]
            at = u * R + (o * SK) // BLK * BLK
            gcp[o, BLK + u:BLK + u + 1, :] = flows[:, at:at + BLK]
    for at in sorted(cc, key=lambda at: -at[1]):
        cc[at].start()
    chain(0, 2)
    chain(1, 2)
    finish(0)
    finish(1)

    for w in both:
        fx[w].wait_recv()
        gb_ref[2 * side(w) + other] = got[w, :SK, :]
        gc_ref[2 * side(w) + other] = got[w, SK:BLK, :]

    def pick(flag, a, b):
        return jnp.where(jnp.full((1, BLK), flag) == 0, a, b)

    ours = [fin[w, core, BLK:BLK + 1, :] for w in both]
    rest = [got[w, BLK:BLK + 1, :] for w in both]
    ours = [pick(ky, ours[0], ours[1]), pick(ky, ours[1], ours[0])]
    rest = [pick(ky, rest[0], rest[1]), pick(ky, rest[1], rest[0])]
    flows = jnp.concatenate(
        [pick(core, x, y) for y_hi in both for x, y in ((ours[y_hi], rest[y_hi]), (rest[y_hi], ours[y_hi]))],
        axis=0,
    )
    gl_ref[...] = jnp.where(jnp.full((S, SK), core) == 0, flows[:, :SK], flows[:, SK:])

    for copies in list(kp.values()) + list(bp.values()) + uc + dc:
        for copy in copies:
            copy.wait_send()
    for copy in list(kf.values()) + list(bf.values()) + stats + list(cc.values()) + fx:
        copy.wait_send()
    for copy in (qx[0], cx[0], hx):
        copy.wait_send()


def shards(nq, nk, queries, keys, c_proj, b_proj, decay_rate, doc_ids):
    S, R, D = queries.shape
    NB = decay_rate.shape[1] // BLK
    rates = decay_rate.reshape(S, NB, BLK).transpose(1, 0, 2).reshape(NB * S, BLK)
    RR = 2 * R
    pay = BLK + 8
    vmem = pl.BlockSpec(memory_space=pltpu.VMEM)
    dma = pltpu.SemaphoreType.DMA
    f32, bf16 = jnp.float32, jnp.bfloat16
    return pl.pallas_call(
        functools.partial(kernel, nq, nk),
        out_shape=(
            jax.ShapeDtypeStruct((S, SK, D), f32),
            jax.ShapeDtypeStruct((S, SK, D), f32),
            jax.ShapeDtypeStruct((S, SK), f32),
        ),
        in_specs=[pl.BlockSpec(memory_space=pltpu.HBM)] * 5 + [pl.BlockSpec(memory_space=pltpu.SMEM)],
        out_specs=(vmem, vmem, vmem),
        scratch_shapes=[
            pltpu.VMEM((2, R, D), bf16),
            pltpu.VMEM((2, R, D), bf16),
            pltpu.VMEM((SLOTS, WAVES, 2, SK, D), bf16),
            pltpu.VMEM((SLOTS, WAVES, 2, SK, D), bf16),
            pltpu.VMEM((SLOTS, WAVES, BLK, RR), f32),
            pltpu.VMEM((SLOTS, WAVES, 1, RR), f32),
            pltpu.VMEM((SLOTS, WAVES, 1, RR), f32),
            pltpu.VMEM((SLOTS, WAVES, 1, RR), f32),
            pltpu.VMEM((NB, BLK), f32),
            pltpu.VMEM((SLOTS, WAVES, BLK, BLK), f32),
            pltpu.VMEM((D, RR), f32),
            pltpu.VMEM((8, RR), f32),
            pltpu.VMEM((SLOTS, WAVES, pay, D), f32),
            pltpu.VMEM((3, WAVES, pay, D), f32),
            pltpu.VMEM((3, WAVES, pay, D), f32),
            pltpu.VMEM((nk, pay, D), f32),
            pltpu.VMEM((nk // 2, 2, pay, D), f32),
            pltpu.VMEM((2, 1, RR), f32),
            pltpu.VMEM((nk // 2, 2, 1, RR), f32),
            pltpu.VMEM((WAVES, 2, pay, D), f32),
            pltpu.VMEM((WAVES, pay, D), f32),
            pltpu.VMEM((pay, D), f32),
            pltpu.VMEM((NB * S, BLK), f32),
            pltpu.VMEM((SLOTS, WAVES, BLK, RR), f32),
            pltpu.VMEM((SLOTS, WAVES, BLK, RR), f32),
        ]
        + [dma((5,))]
        + [dma((SLOTS, WAVES, 2))] * 4
        + [dma] * 6
        + [dma((nk // 2,))] * 2
        + [dma((3, WAVES))] * 4
        + [dma((nk // 2, 2))] * 2
        + [dma((WAVES,))] * 2,
        compiler_params=pltpu.CompilerParams(
            collective_id=0, has_side_effects=True, vmem_limit_bytes=63 * 1024 * 1024
        ),
    )(queries, c_proj, keys, b_proj, rates, doc_ids)


def solution(mesh):
    placed = (
        P(None, "qb", None),
        P(None, ("qb", "kb"), None),
        P(None, "qb", None),
        P(None, ("qb", "kb"), None),
        P(),
        P(),
    )
    return jax.shard_map(
        functools.partial(shards, mesh.shape["qb"], mesh.shape["kb"]),
        mesh=mesh,
        in_specs=placed,
        out_specs=(P(None, ("qb", "kb"), None), P(None, ("qb", "kb"), None), P(None, ("qb", "kb"))),
        check_vma=False,
    )
```

```python
import functools
import math

import jax
import jax.numpy as jnp
from jax import lax
from jax.experimental import pallas as pl
from jax.experimental.pallas import tpu as pltpu
from jax.sharding import PartitionSpec as P

MESH = pl.DeviceIdType.MESH
HIGHEST = lax.Precision.HIGHEST
NEG = -1e30
SK = 64
BLK = 128
SLOTS = 7
WAVES = 2


def nt(a, b, precision=None):
    return lax.dot_general(
        a, b, (((1,), (1,)), ((), ())), preferred_element_type=jnp.float32, precision=precision
    )


def kernel(
    nq, nk,
    q_ref, c_ref, k_ref, b_ref, rate_ref, doc_ref,
    gc_ref, gb_ref, gl_ref,
    qbuf, cbuf, kbuf, bbuf, ebuf, mbuf, lbuf, fbuf, lcs, lckb, gct, rf, gp, up, dn, gcp, gcr, st, str_, fin, got, held, rbuf, mixbuf, decbuf,
    ls, ks, kr, bs, br, qs, qr, cs, cr, hs, hr, sts, strs, us, ur, ds, dr, gcs, gcrs, fs, fr,
):
    S, R, D = q_ref.shape
    RB = R // BLK
    NB = nq * RB
    RR = 2 * R
    nx = nk // 2
    npair = nq // 2
    qb = lax.axis_index("qb")
    kb = lax.axis_index("kb")
    pr = qb // 2
    core = qb % 2
    other = 1 - core
    kx = kb // 2
    ky = kb % 2
    both = range(2)
    me = 2 * ky + core

    def side(g):
        return ky if g == 0 else 1 - ky

    def dev(step, which, g=0):
        return (((pr + step + npair) % npair) * 2 + which, kx * 2 + side(g))

    sibling = dev(0, other)
    crowd = [(dx, g) for dx in range(nx) for g in both if dx or g]

    def peer(dx, g):
        return (qb, ((kx + dx) % nx) * 2 + side(g))

    barrier = pltpu.get_barrier_semaphore()
    partners = [dev(step, u, g) for step in (1, -1, 6, -6) for u in both for g in both]
    partners += [sibling, dev(0, other, 1)] + [peer(dx, g) for dx, g in crowd]
    for to in partners:
        pl.semaphore_signal(barrier, inc=1, device_id=to, device_id_type=MESH)

    def rc(src, dst, ssem, rsem, to):
        return pltpu.make_async_remote_copy(
            src_ref=src, dst_ref=dst, send_sem=ssem, recv_sem=rsem, device_id=to, device_id_type=MESH
        )

    def own_push(own, buf, ssem, rsem):
        push, land = {}, {}
        for e in (0, 1, 6):
            for g in both:
                push[e, g], land[e, g] = [], []
                for v in both:
                    if e == g == v == 0:
                        continue
                    which = (core + v) % 2
                    push[e, g].append(rc(
                        own.at[2 * side(g) + which], buf.at[e, g, core],
                        ssem.at[e, g, v], rsem.at[e, g, v], dev(e, which, g),
                    ))
                    land[e, g].append(rc(
                        buf.at[e, g, which], buf.at[e, g, which],
                        ssem.at[e, g, v], rsem.at[e, g, v], dev(-e, which, g),
                    ))
        return push, land

    def pass_on(buf, ssem, rsem):
        out = {}
        for e, f, step in ((2, 1, 1), (3, 2, 1), (5, 6, -1), (4, 5, -1)):
            for g in both:
                out[e, g] = rc(
                    buf.at[f, g], buf.at[e, g], ssem.at[e, g, 0], rsem.at[e, g, 0], dev(step, core)
                )
        return out

    def swap(own, buf, ssem, rsem):
        return (
            rc(own.at[2 * ky + other], buf.at[core], ssem, rsem, sibling),
            rc(buf.at[other], buf.at[other], ssem, rsem, sibling),
        )

    kp, kl = own_push(k_ref, kbuf, ks, kr)
    bp, bl = own_push(b_ref, bbuf, bs, br)
    kf, bf = pass_on(kbuf, ks, kr), pass_on(bbuf, bs, br)
    qx = swap(q_ref, qbuf, qs, qr)
    cx = swap(c_ref, cbuf, cs, cr)

    local = [
        pltpu.make_async_copy(src, dst, ls.at[i])
        for i, (src, dst) in enumerate((
            (k_ref.at[me], kbuf.at[0, 0, core]),
            (q_ref.at[me], qbuf.at[core]),
            (rate_ref, rbuf),
            (b_ref.at[me], bbuf.at[0, 0, core]),
            (c_ref.at[me], cbuf.at[core]),
        ))
    ]
    for copy in local:
        copy.start()

    lane = lax.broadcasted_iota(jnp.int32, (1, BLK), 1)
    sub = lax.broadcasted_iota(jnp.int32, (BLK, BLK), 0)

    def key_block(e, g, u):
        j = (pr - e + npair) % npair
        return (2 * j + u) * RB + ((kx * 2 + side(g)) * SK) // BLK

    def key_columns(e, w):
        first = lcs[pl.ds(key_block(e, w, 0), 1), :]
        second = lcs[pl.ds(key_block(e, w, 1), 1), :]
        low = jnp.concatenate([first[:, :SK], second[:, :SK]], axis=1)
        high = jnp.concatenate([first[:, SK:], second[:, SK:]], axis=1)
        row = jnp.where(jnp.full((1, BLK), side(w)) == 0, low, high)
        lckb[e, w] = jnp.broadcast_to(row, (BLK, BLK)).T

    pl.semaphore_wait(barrier, len(partners))

    def push(copies, e, w):
        for copy in copies[e, w]:
            copy.start()

    for g in both:
        push(kp, 6, g)
    for g in both:
        push(kp, 1, g)
    for g in both:
        push(kp, 0, g)
    qx[0].start()
    for g in both:
        push(bp, 6, g)
    for g in both:
        push(bp, 1, g)
    for g in both:
        push(bp, 0, g)
    cx[0].start()

    local[2].wait()
    row = lax.broadcasted_iota(jnp.int32, (NB, NB * S), 0)
    col = lax.broadcasted_iota(jnp.int32, (NB, NB * S), 1)
    ours = (col % S) == me
    blk = col // S
    base = pr * 2 * RB
    rates = jnp.dot(
        (ours & (blk == row)).astype(jnp.float32), rbuf[...],
        preferred_element_type=jnp.float32, precision=HIGHEST,
    )
    after = (ours & (blk >= base) & (blk < row)).astype(jnp.float32)
    before = (ours & (blk >= row) & (blk < base)).astype(jnp.float32)
    blocks = jnp.dot(
        after - before, rbuf[...], preferred_element_type=jnp.float32, precision=HIGHEST
    )
    row = lax.broadcasted_iota(jnp.int32, (BLK, BLK), 0)
    col = lax.broadcasted_iota(jnp.int32, (BLK, BLK), 1)
    within = jnp.dot(
        rates, (row <= col).astype(jnp.float32), preferred_element_type=jnp.float32, precision=HIGHEST
    )
    lcs[...] = -(within + jnp.sum(blocks, axis=1, keepdims=True))

    for e in range(SLOTS):
        for w in range(WAVES):
            key_columns(e, w)

    gct[...] = jnp.zeros_like(gct)
    rf[...] = jnp.zeros_like(rf)
    gp[:, :, BLK:, :] = jnp.zeros((SLOTS, WAVES, 8, D), jnp.float32)
    gcp[:, BLK:, :] = jnp.zeros((nk, 8, D), jnp.float32)
    fin[:, :, BLK:, :] = jnp.zeros((WAVES, 2, 8, D), jnp.float32)

    def biases(e, w, r):
        rd = doc_ref[me, pr * 2 * RB + r]
        out = []
        for u in range(2):
            same = doc_ref[me, key_block(e, w, u)] == rd
            if e:
                same = same & (pr >= e)
            out.append(jnp.where(same, 0.0, NEG).astype(jnp.float32))
        return out

    def causal(w, r):
        kpos = (2 * pr) * R + (kx * 2 + side(w)) * SK + jnp.where(sub >= SK, sub - SK + R, sub)
        rpos = pr * RR + r * BLK + lane
        return kpos <= rpos

    scale = (D ** -0.5) * math.log2(math.e)

    def first_pass(e, w):
        every = nt(kbuf[e, w].reshape(BLK, D), qbuf[...].reshape(RR, D)) * scale
        for r in range(2 * RB):
            cols = slice(r * BLK, (r + 1) * BLK)
            sc = every[:, cols]
            if e == 0:
                sc = jnp.where(causal(w, r), sc, NEG)
            bias = biases(e, w, r)
            halves = [sc[:SK], sc[SK:]]
            top = jnp.maximum(
                jnp.max(halves[0], axis=0, keepdims=True) + bias[0],
                jnp.max(halves[1], axis=0, keepdims=True) + bias[1],
            )
            total = jnp.zeros((1, BLK), jnp.float32)
            for u in range(2):
                ex = jnp.exp2(halves[u] - jnp.maximum(top, NEG - 2.0 * bias[u]))
                ebuf[e, w, u * SK:(u + 1) * SK, cols] = ex
                total += jnp.sum(ex, axis=0, keepdims=True)
            mbuf[e, w, :, cols] = top
            lbuf[e, w, :, cols] = total

    def mix_pass(e, w):
        kcol = lckb[e, w]
        products = nt(bbuf[e, w].reshape(BLK, D), cbuf[...].reshape(RR, D))
        for r in range(2 * RB):
            cols = slice(r * BLK, (r + 1) * BLK)
            bias = biases(e, w, r)
            rows = lcs[pl.ds(pr * 2 * RB + r, 1), :]
            spread = jnp.concatenate(
                [(rows + bias[0]) - kcol[:SK], (rows + bias[1]) - kcol[SK:]], axis=0
            )
            if e == 0:
                spread = jnp.where(causal(w, r), spread, NEG)
            decay = jnp.exp(spread)
            decbuf[e, w, :, cols] = decay
            mixbuf[e, w, :, cols] = products[:, cols] * decay

    def passed(land, forward, *slots):
        for w in both:
            for e in slots:
                if e in (0, 1, 6):
                    for copy in land[e, w]:
                        copy.wait_recv()
                else:
                    forward[e, w].wait_recv()
                follow = {1: 2, 2: 3, 6: 5, 5: 4}.get(e)
                if follow is not None:
                    forward[follow, w].start()

    stats = [rc(st, str_.at[o], sts.at[o], strs.at[o], peer(o, 0)) for o in range(1, nx)]
    every = [(e, w) for e in range(SLOTS) for w in both]

    for w in both:
        for copy in kl[0, w]:
            copy.wait_recv()
    qx[1].wait_recv()
    local[0].wait()
    local[1].wait()
    for w in both:
        first_pass(0, w)
    passed(kl, kf, 1, 6)
    for e in (1, 6):
        for w in both:
            first_pass(e, w)
    passed(bl, bf, 1, 6)
    passed(bl, bf, 0)
    cx[1].wait_recv()
    local[3].wait()
    local[4].wait()
    passed(kl, kf, 2, 5)
    for e in (2, 5):
        for w in both:
            first_pass(e, w)
    passed(bl, bf, 2, 5)
    for e in (0, 1, 6):
        for w in both:
            mix_pass(e, w)
    passed(kl, kf, 3, 4)
    for e in (3, 4):
        for w in both:
            first_pass(e, w)
    top = mbuf[0, 0]
    for at in every:
        top = jnp.maximum(top, mbuf[at])
    total = jnp.zeros_like(top)
    for at in every:
        total += lbuf[at] * jnp.exp2(mbuf[at] - top)
    st[0] = top
    st[1] = total
    for copy in stats:
        copy.start()
    for w in both:
        for e in (3, 4):
            bf[e, w].wait_recv()
            mix_pass(e, w)
    for w in both:
        mix_pass(2, w)
        mix_pass(5, w)
    for copy in stats:
        copy.wait_recv()
    best = top
    for o in range(1, nx):
        best = jnp.maximum(best, str_[o, 0])
    whole = total * jnp.exp2(top - best)
    for o in range(1, nx):
        whole += str_[o, 1] * jnp.exp2(str_[o, 0] - best)
    for at in every:
        fbuf[at] = jnp.exp2(mbuf[at] - best) / whole

    ones = jnp.ones((8, BLK), jnp.float32)

    def second_pass(e, w):
        bt = bbuf[e, w].reshape(BLK, D).T
        weights = []
        gathered = jnp.zeros((BLK, BLK), jnp.float32)
        for r in range(2 * RB):
            cols = slice(r * BLK, (r + 1) * BLK)
            mixing = mixbuf[e, w, :, cols]
            gap = mixing - ebuf[e, w, :, cols] * fbuf[e, w, :, cols]
            flow = gap * mixing
            weights.append((gap * decbuf[e, w, :, cols]).astype(jnp.bfloat16))
            gathered += flow
            rf[:, cols] += jnp.sum(flow.reshape(BLK // 8, 8, BLK), axis=0)
        wide = jnp.concatenate(weights, axis=1)
        gct[...] += jnp.dot(bt, wide, preferred_element_type=jnp.float32)
        gp[e, w, :BLK, :] = jnp.dot(wide, cbuf[...].reshape(RR, D), preferred_element_type=jnp.float32)
        gp[e, w, BLK:BLK + 1, :] = nt(ones, gathered, HIGHEST)[0:1]

    uc = [
        [
            rc(gp.at[e, w], up.at[i, w], us.at[i, w], ur.at[i, w], dev(-1, core, w if e == 1 else 0))
            for w in both
        ]
        for i, e in enumerate((3, 2, 1))
    ]
    dc = [
        [
            rc(
                gp.at[e, w], dn.at[i, w], ds.at[i, w], dr.at[i, w],
                dev(-6, core, w) if e == 6 else dev(1, core),
            )
            for w in both
        ]
        for i, e in enumerate((4, 5, 6))
    ]
    cc = {
        (dx, g): rc(
            gcp.at[((kx + dx) % nx) * 2 + side(g)], gcr.at[dx, g],
            gcs.at[dx, g], gcrs.at[dx, g], peer(dx, g),
        )
        for dx, g in crowd
    }
    fx = [rc(fin.at[w, other], got.at[w], fs.at[w], fr.at[w], sibling) for w in both]
    hx = rc(gp.at[0, 1], held, hs, hr, dev(0, core, 1))

    def chain(e, copies, landed, w, step):
        if step:
            copies[step - 1][w].wait_recv()
            gp[e, w] = gp[e, w] + landed[step - 1, w]
        copies[step][w].start()

    def send_dn(w, step):
        chain(4 + step, dc, dn, w, step)

    def send_up(w, step):
        chain(3 - step, uc, up, w, step)

    def finish(w):
        uc[2][w].wait_recv()
        dc[2][w].wait_recv()
        if w:
            hx.wait_recv()
            bsum = held[...]
        else:
            bsum = gp[0, 0]
        bsum = (bsum + (up[2, w] + dn[2, w])) * 2.0
        for dx in range(nx):
            if dx or w:
                cc[dx, w].wait_recv()
        csum = gcr[0, 1] if w else gcp[kb]
        for dx in range(1, nx):
            csum += gcr[dx, w]
        csum = csum * 2.0
        flows = []
        for u in range(2):
            fin[w, u, :SK, :] = bsum[u * SK:(u + 1) * SK]
            fin[w, u, SK:BLK, :] = csum[u * SK:(u + 1) * SK]
            rowf = csum[BLK + u:BLK + u + 1]
            rowf = jnp.where(jnp.full((1, SK), ky) == 0, rowf[:, :SK], rowf[:, SK:])
            flows.append(rowf - bsum[BLK:BLK + 1, u * SK:(u + 1) * SK])
        flows = jnp.concatenate(flows, axis=1)
        for u in range(2):
            fin[w, u, BLK:BLK + 1, :] = flows
        fx[w].start()
        gb_ref[2 * side(w) + core] = fin[w, core, :SK, :]
        gc_ref[2 * side(w) + core] = fin[w, core, SK:BLK, :]

    for w in both:
        second_pass(4, w)
        send_dn(w, 0)
    for w in both:
        second_pass(3, w)
        send_up(w, 0)
    for e in (5, 2, 6):
        for w in both:
            second_pass(e, w)
    for w in both:
        send_dn(w, 1)
        second_pass(1, w)
    for w in both:
        send_up(w, 1)
    second_pass(0, 1)
    hx.start()
    second_pass(0, 0)
    turned = gct[...].T
    flows = jnp.sum(rf[...], axis=0, keepdims=True)
    for o in range(nk):
        for u in range(2):
            at = u * R + o * SK
            gcp[o, u * SK:(u + 1) * SK, :] = turned[at:at + SK]
            at = u * R + (o * SK) // BLK * BLK
            gcp[o, BLK + u:BLK + u + 1, :] = flows[:, at:at + BLK]
    for at in sorted(cc, key=lambda at: -at[1]):
        cc[at].start()
    for w in both:
        send_dn(w, 2)
    for w in both:
        send_up(w, 2)
    finish(0)
    finish(1)

    for w in both:
        fx[w].wait_recv()
        gb_ref[2 * side(w) + other] = got[w, :SK, :]
        gc_ref[2 * side(w) + other] = got[w, SK:BLK, :]

    def pick(flag, a, b):
        return jnp.where(jnp.full((1, BLK), flag) == 0, a, b)

    ours = [fin[w, core, BLK:BLK + 1, :] for w in both]
    rest = [got[w, BLK:BLK + 1, :] for w in both]
    ours = [pick(ky, ours[0], ours[1]), pick(ky, ours[1], ours[0])]
    rest = [pick(ky, rest[0], rest[1]), pick(ky, rest[1], rest[0])]
    flows = jnp.concatenate(
        [pick(core, x, y) for y_hi in both for x, y in ((ours[y_hi], rest[y_hi]), (rest[y_hi], ours[y_hi]))],
        axis=0,
    )
    gl_ref[...] = jnp.where(jnp.full((S, SK), core) == 0, flows[:, :SK], flows[:, SK:])

    for copies in list(kp.values()) + list(bp.values()) + uc + dc:
        for copy in copies:
            copy.wait_send()
    for copy in list(kf.values()) + list(bf.values()) + stats + list(cc.values()) + fx:
        copy.wait_send()
    for copy in (qx[0], cx[0], hx):
        copy.wait_send()


def shards(nq, nk, queries, keys, c_proj, b_proj, decay_rate, doc_ids):
    S, R, D = queries.shape
    NB = decay_rate.shape[1] // BLK
    rates = decay_rate.reshape(S, NB, BLK).transpose(1, 0, 2).reshape(NB * S, BLK)
    RR = 2 * R
    pay = BLK + 8
    vmem = pl.BlockSpec(memory_space=pltpu.VMEM)
    dma = pltpu.SemaphoreType.DMA
    f32, bf16 = jnp.float32, jnp.bfloat16
    return pl.pallas_call(
        functools.partial(kernel, nq, nk),
        out_shape=(
            jax.ShapeDtypeStruct((S, SK, D), f32),
            jax.ShapeDtypeStruct((S, SK, D), f32),
            jax.ShapeDtypeStruct((S, SK), f32),
        ),
        in_specs=[pl.BlockSpec(memory_space=pltpu.HBM)] * 5 + [pl.BlockSpec(memory_space=pltpu.SMEM)],
        out_specs=(vmem, vmem, vmem),
        scratch_shapes=[
            pltpu.VMEM((2, R, D), bf16),
            pltpu.VMEM((2, R, D), bf16),
            pltpu.VMEM((SLOTS, WAVES, 2, SK, D), bf16),
            pltpu.VMEM((SLOTS, WAVES, 2, SK, D), bf16),
            pltpu.VMEM((SLOTS, WAVES, BLK, RR), f32),
            pltpu.VMEM((SLOTS, WAVES, 1, RR), f32),
            pltpu.VMEM((SLOTS, WAVES, 1, RR), f32),
            pltpu.VMEM((SLOTS, WAVES, 1, RR), f32),
            pltpu.VMEM((NB, BLK), f32),
            pltpu.VMEM((SLOTS, WAVES, BLK, BLK), f32),
            pltpu.VMEM((D, RR), f32),
            pltpu.VMEM((8, RR), f32),
            pltpu.VMEM((SLOTS, WAVES, pay, D), f32),
            pltpu.VMEM((3, WAVES, pay, D), f32),
            pltpu.VMEM((3, WAVES, pay, D), f32),
            pltpu.VMEM((nk, pay, D), f32),
            pltpu.VMEM((nk // 2, 2, pay, D), f32),
            pltpu.VMEM((2, 1, RR), f32),
            pltpu.VMEM((nk // 2, 2, 1, RR), f32),
            pltpu.VMEM((WAVES, 2, pay, D), f32),
            pltpu.VMEM((WAVES, pay, D), f32),
            pltpu.VMEM((pay, D), f32),
            pltpu.VMEM((NB * S, BLK), f32),
            pltpu.VMEM((SLOTS, WAVES, BLK, RR), f32),
            pltpu.VMEM((SLOTS, WAVES, BLK, RR), f32),
        ]
        + [dma((5,))]
        + [dma((SLOTS, WAVES, 2))] * 4
        + [dma] * 6
        + [dma((nk // 2,))] * 2
        + [dma((3, WAVES))] * 4
        + [dma((nk // 2, 2))] * 2
        + [dma((WAVES,))] * 2,
        compiler_params=pltpu.CompilerParams(
            collective_id=0, has_side_effects=True, vmem_limit_bytes=63 * 1024 * 1024
        ),
    )(queries, c_proj, keys, b_proj, rates, doc_ids)


def solution(mesh):
    placed = (
        P(None, "qb", None),
        P(None, ("qb", "kb"), None),
        P(None, "qb", None),
        P(None, ("qb", "kb"), None),
        P(),
        P(),
    )
    return jax.shard_map(
        functools.partial(shards, mesh.shape["qb"], mesh.shape["kb"]),
        mesh=mesh,
        in_specs=placed,
        out_specs=(P(None, ("qb", "kb"), None), P(None, ("qb", "kb"), None), P(None, ("qb", "kb"))),
        check_vma=False,
    )
```
